256 devices in a mesh: ax: 16 (over y_hi, x, core), az: 16 (over z, y_lo).
Axes of the slice: x: 4, y: 4 (y_hi: 2, y_lo: 2; y = y_hi * 2 + y_lo), z: 8, core: 2. Of those that a mesh axis runs over, the one named last changes fastest.
Arguments:
- adjoint: float32 [5, 2, 256, 128, 128], P(None, None, 'ax', 'az'), may hold values from -6 to 6
- mean_flow: float32 [3, 256, 128, 128], P(None, 'ax', 'az'), may hold values from 0.5 to 1.5
- forcing: float32 [2, 256, 128, 128], P(None, 'ax', 'az'), may hold values from -6 to 6
- tke: float32 [256, 128, 128], P('ax', 'az'), may hold values from 0.03 to 0.3
- half_width: int32 [256, 128, 128], P('ax', 'az'), may hold values from 2 to 16
- start: int32 [1], replicated, may hold values from 0 to 1792
Outputs:
- green: float32 [5, 2, 256, 128, 128], P(None, None, 'ax', 'az')
- intensity: float32 [256, 128, 128], P('ax', 'az')
The draws below stay inside these ranges and needn't reach their ends.
All inputs are finite; a program needn't handle non-finite values.
Results may differ from the reference program's by a relative error of at most 0.00002.
Values sent between devices are 32-bit elements; how exact they have to be, the bound alone decides.
A program may use at most 64 MiB of HBM per device.

```python
import math
import jax
import jax.numpy as jnp

NR = 128
SEP = 16
ITERS = 2
NAXIAL = 2048
NXW = 256
NTH = 128


def place_ends(entries, rng, least, high):
    spot = [jax.random.randint(jax.random.fold_in(rng, axis), (), 0, length) for axis, length in enumerate(entries.shape)]
    longest = entries.shape.index(max(entries.shape))
    beside = spot[:longest] + [(spot[longest] + 1) % entries.shape[longest]] + spot[longest + 1:]
    return entries.at[tuple(spot)].set(least).at[tuple(beside)].set(high)


def levels(own_key, shape, cuts, low, largest):
    loudness, own = 1.0, jax.random.fold_in(own_key, 6)
    for position, shards_of in cuts:
        draws = jnp.exp(jax.random.uniform(jax.random.fold_in(own, position), (shards_of,), jnp.float32, low / len(cuts), largest / len(cuts)))
        loudness = loudness * jnp.repeat(draws, shape[position] // shards_of).reshape([-1 if axis == position else 1 for axis in range(len(shape))])
    return loudness


def bell_draw(rng, extent, deviation, limit, split=(), kind=jnp.bfloat16):
    values = deviation * jax.random.normal(rng, extent, jnp.float32)
    if split:
        values = values * levels(rng, extent, split, -0.22, 0.18)
    return jnp.clip(values, -limit, limit).astype(kind)


def setup_inputs(seed: int = 0) -> dict:
    arg_keys = jax.random.split(jax.random.key(seed), 7)
    return {
        "adjoint": bell_draw(arg_keys[0], (5, 2, NXW, NTH, NR), 1.0, 6.0, ((2, 16), (3, 16)), jnp.float32),
        "mean_flow": jnp.clip(0.5 + 1.0 * jax.random.uniform(arg_keys[1], (3, NXW, NTH, NR), jnp.float32) ** levels(arg_keys[1], (3, NXW, NTH, NR), ((1, 16), (2, 16)), -0.2, 0.2), 0.5, 1.5),
        "forcing": bell_draw(arg_keys[2], (2, NXW, NTH, NR), 1.0, 6.0, ((1, 16), (2, 16)), jnp.float32),
        "tke": jnp.clip(jnp.exp(math.log(0.3) - 2.3025852 * jax.random.uniform(arg_keys[3], (NXW, NTH, NR), jnp.float32) ** levels(arg_keys[3], (NXW, NTH, NR), ((0, 16), (1, 16)), -0.2, 0.2)), 0.03, 0.3),
        "half_width": place_ends(jax.random.randint(arg_keys[4], (NXW, NTH, NR), 2, SEP + 1), jax.random.fold_in(arg_keys[4], 1), 2, SEP).astype(jnp.int32),
        "start": jax.random.randint(arg_keys[5], (1,), 0, NAXIAL - NXW + 1).astype(jnp.int32),
    }


FREQUENCY = 0.7
SECTION_WEIGHTS = (1.0 / 3.0, 0.5, 1.0)


def coefficients(mean_flow):
    return jnp.stack([mean_flow[0], mean_flow[1], mean_flow[1] * mean_flow[2], 1.0 / mean_flow[1]])


def axial_flux(state, coeffs):
    speed = coeffs[0][None]
    density = coeffs[1][None]
    stiff = coeffs[2][None]
    inverse = coeffs[3][None]
    return jnp.stack([speed * state[0], density * state[0] + speed * state[1] + stiff * state[4], speed * state[2], speed * state[3], state[1] * inverse + speed * state[4]])


def shared_flux(state, coeffs):
    return coeffs[1][None] * state[0] + coeffs[2][None] * state[4]


def reference(adjoint, mean_flow, forcing, tke, half_width, start):
    azimuth_step = 2 * math.pi / NTH
    radius = jnp.arange(NR, dtype=jnp.float32) + 0.5
    tstep = 0.8 / (2.0 + 1.0 / (radius * azimuth_step))
    axial_pos = (start[0] + jnp.arange(NXW, dtype=jnp.int32)).astype(jnp.float32)
    damping = (0.5 * (axial_pos + 0.5) / NAXIAL)[:, None, None]
    coeffs = coefficients(mean_flow)

    def right_side(state):
        flux_x = jnp.pad(axial_flux(state, coeffs), ((0, 0), (0, 0), (1, 1), (0, 0), (0, 0)))
        shared = shared_flux(state, coeffs)
        lateral = jnp.stack([shared, state[3] * coeffs[3][None]])
        wrapped = jnp.concatenate([lateral[:, :, :, -1:], lateral, lateral[:, :, :, :1]], axis=3)
        radial = jnp.stack([shared, state[2] * coeffs[3][None]])
        mirrored = jnp.roll(radial[..., 0], NTH // 2, axis=3)
        scaled = radius * radial
        padded = jnp.concatenate([0.5 * mirrored[..., None], scaled, jnp.zeros_like(scaled[..., :1])], axis=-1)
        along_x = (flux_x[:, :, 2:] - flux_x[:, :, :-2]) * 0.5
        along_t = (wrapped[:, :, :, 2:] - wrapped[:, :, :, :-2]) * (0.5 / (azimuth_step * radius))
        along_r = (padded[..., 2:] - padded[..., :-2]) * (0.5 / radius)
        components = jnp.stack([along_x[0], along_x[1], along_x[2] + along_r[0], along_x[3] + along_t[0], along_x[4] + along_r[1] + along_t[1]])
        summed = components - damping * state + FREQUENCY * jnp.stack([state[:, 1], -state[:, 0]], axis=1)
        return summed.at[4].add(forcing)

    state = adjoint
    for outer in range(ITERS):
        base = state
        for section_weight in SECTION_WEIGHTS:
            state = base + section_weight * (tstep * right_side(state))
    pressure = state[4]
    widened = jnp.pad(pressure, ((0, 0), (SEP, SEP), (0, 0), (0, 0)))
    length = half_width.astype(jnp.float32)
    inverse = 1.0 / (length * length)
    summed = jnp.zeros(pressure.shape[1:], jnp.float32)
    for shift_by in range(-SEP, SEP + 1):
        shifted = widened[:, SEP + shift_by:SEP + shift_by + NXW]
        weight = jnp.exp(-(shift_by * shift_by) * inverse)
        summed = summed + weight * (pressure[0] * shifted[0] + pressure[1] * shifted[1])
    return state, tke * summed
```

```python
import functools
import math

import jax
import jax.numpy as jnp
from jax import lax
from jax.experimental import pallas as pl
from jax.experimental.pallas import tpu as pltpu
from jax.sharding import PartitionSpec as P

SEP = 16
SECTIONS = 6
NAXIAL = 2048
FREQUENCY = 0.7
MESH = pl.DeviceIdType.MESH
CHUNK = 4


def kernel(
    n_ax, n_az,
    start, adjoint, mean_flow, forcing, tke, half_width,
    green, intensity,
    state, partial, coef, force, sigma, amp, width, weights, flow, result,
    flux_x, flux_l, send_x, recv_x, recv_t, send_o, recv_o, pressure,
    load_sem, store_sem, x_send, x_recv, t_send, t_recv, o_send, o_recv, p_send, p_recv,
):
    cells, sector, radial = state.shape[3], state.shape[4], state.shape[5]
    ax, az = lax.axis_index("ax"), lax.axis_index("az")
    left, right = ax - 1, ax + 1
    below, above = lax.rem(az + n_az - 1, n_az), lax.rem(az + 1, n_az)
    opposite = lax.rem(az + n_az // 2, n_az)
    has_left, has_right = ax > 0, ax < n_ax - 1

    loads = [
        pltpu.make_async_copy(src, dst, load_sem.at[n])
        for n, (src, dst) in enumerate(
            [(mean_flow, flow), (adjoint, state.at[0]), (forcing, force), (half_width, width), (tke, amp)]
        )
    ]
    for load in loads:
        load.start()

    barrier = pltpu.get_barrier_semaphore()
    for k in (below, above, opposite):
        pl.semaphore_signal(barrier, inc=1, device_id=(ax, k), device_id_type=MESH)

    @pl.when(has_left)
    def _():
        pl.semaphore_signal(barrier, inc=1, device_id=(left, az), device_id_type=MESH)

    @pl.when(has_right)
    def _():
        pl.semaphore_signal(barrier, inc=1, device_id=(right, az), device_id_type=MESH)

    step_t = 2 * math.pi / (sector * n_az)
    lane = lax.broadcasted_iota(jnp.int32, (sector, radial), 1)
    row = lax.broadcasted_iota(jnp.int32, (sector, radial), 0)
    radius = lane.astype(jnp.float32) + 0.5
    tau = 0.8 / (2.0 + 1.0 / (radius * step_t))
    turn = 0.5 / (step_t * radius)
    outward = jnp.where(lane == radial - 1, 0.0, 0.5 * (radius + 1.0) / radius)
    inward = jnp.where(lane == 0, 0.0, 0.5 * (radius - 1.0) / radius)
    up = jnp.where(row == sector - 1, 0.0, turn)
    down = jnp.where(row == 0, 0.0, turn)
    edge = jnp.where(row == 0, -turn, turn)
    is_edge = (row == 0) | (row == sector - 1)
    is_axis = lane == 0

    first = start[0] + ax * cells
    pos = first + lax.broadcasted_iota(jnp.int32, (cells, sector, radial), 0)
    sigma[...] = 0.5 * (pos.astype(jnp.float32) + 0.5) / NAXIAL

    flux_x[:, :, 0] = jnp.zeros((5, 2, sector, radial), jnp.float32)
    flux_x[:, :, cells + 1] = jnp.zeros((5, 2, sector, radial), jnp.float32)

    @pl.when(jnp.logical_not(has_left))
    def _():
        pressure[:, 0:cells] = jnp.zeros((2, cells, sector, radial), jnp.float32)

    @pl.when(jnp.logical_not(has_right))
    def _():
        pressure[:, 2 * cells : 3 * cells] = jnp.zeros((2, cells, sector, radial), jnp.float32)

    def t_copy(s, way):
        source, target, who = ((sector - 1, 0, above), (0, sector - 1, below))[way]
        return pltpu.make_async_remote_copy(
            src_ref=flux_l.at[s, pl.ds(0, 4), :, source],
            dst_ref=recv_t.at[s, :, :, target],
            send_sem=t_send.at[s, way], recv_sem=t_recv.at[s, way],
            device_id=(ax, who), device_id_type=MESH,
        )

    def x_copy(s, way):
        return pltpu.make_async_remote_copy(
            src_ref=send_x.at[s, way], dst_ref=recv_x.at[s, way],
            send_sem=x_send.at[s, way], recv_sem=x_recv.at[s, way],
            device_id=((right, left)[way], az), device_id_type=MESH,
        )

    def o_copy(s):
        return pltpu.make_async_remote_copy(
            src_ref=send_o.at[s], dst_ref=recv_o.at[s],
            send_sem=o_send.at[s], recv_sem=o_recv.at[s],
            device_id=(ax, opposite), device_id_type=MESH,
        )

    def p_copy(way):
        return pltpu.make_async_remote_copy(
            src_ref=pressure.at[:, pl.ds(cells, cells)],
            dst_ref=pressure.at[:, pl.ds((0, 2 * cells)[way], cells)],
            send_sem=p_send.at[way], recv_sem=p_recv.at[way],
            device_id=((right, left)[way], az), device_id_type=MESH,
        )

    def fluxes(s, i, q, gathered):
        at = pl.ds(i, CHUNK)
        u, rho, stiff, inv = coef[0, at], coef[1, at], coef[2, at], coef[3, at]
        a, b, c, d, e = q
        shared = rho * a + stiff * e
        turned, spread = d * inv, c * inv
        along = (u * a, shared + u * b, u * c, u * d, b * inv + u * e)
        for n, f in enumerate(along):
            flux_x[n, :, pl.ds(i + 1, CHUNK)] = f
            if i == 0:
                send_x[s, 1, n] = f[:, 0]
            if i == cells - CHUNK:
                send_x[s, 0, n] = f[:, CHUNK - 1]
        flux_l[s, 0:2, at] = shared
        flux_l[s, 2:4, at] = turned
        flux_l[s, 4:6, at] = spread
        for part in range(2):
            for n, f in ((part, shared), (part + 2, spread)):
                for k in range(CHUNK):
                    to = n * cells + i + k
                    value = f[part, k] if to == 0 else pltpu.roll(f[part, k], to, 1)
                    gathered = jnp.where(lane == to, value, gathered)
        return gathered

    def send(s):
        o_copy(s).start()
        t_copy(s, 0).start()
        t_copy(s, 1).start()

        @pl.when(has_right)
        def _():
            x_copy(s, 0).start()

        @pl.when(has_left)
        def _():
            x_copy(s, 1).start()

    def weight_of(s):
        third = lax.rem(s, 3)
        return jnp.where(third == 0, 1.0 / 3.0, jnp.where(third == 1, 0.5, 1.0))

    def inner(s):
        source = lax.rem(s, 3)
        scale = weight_of(s) * tau

        def body(t, carry):
            i = t * CHUNK
            at = pl.ds(i, CHUNK)
            damp = sigma[at]
            shared, turned, spread = flux_l[s, 0:2, at], flux_l[s, 2:4, at], flux_l[s, 4:6, at]

            def radially(f):
                return outward * pltpu.roll(f, radial - 1, 3) - inward * pltpu.roll(f, 1, 3)

            def around(f):
                return up * pltpu.roll(f, sector - 1, 2) - down * pltpu.roll(f, 1, 2)

            extra = (None, None, radially(shared), around(shared), radially(spread) + around(turned) + force[:, at])
            for n in range(5):
                q = state[source, n, :, at]
                total = 0.5 * (flux_x[n, :, pl.ds(i + 2, CHUNK)] - flux_x[n, :, at]) - damp * q
                if extra[n] is not None:
                    total = total + extra[n]
                base = state[0, n, :, at]
                partial[n, 0, at] = base[0] + scale * (total[0] + FREQUENCY * q[1])
                partial[n, 1, at] = base[1] + scale * (total[1] - FREQUENCY * q[0])
            return carry

        lax.fori_loop(0, cells // CHUNK, body, 0)

    def receive(s):
        half = 0.5 * weight_of(s) * tau

        @pl.when(has_left)
        def _():
            x_copy(s, 0).wait_recv()
            partial[:, :, 0] = partial[:, :, 0] - half * recv_x[s, 0]

        @pl.when(has_right)
        def _():
            x_copy(s, 1).wait_recv()
            partial[:, :, cells - 1] = partial[:, :, cells - 1] + half * recv_x[s, 1]

        t_copy(s, 0).wait_recv()
        t_copy(s, 1).wait_recv()
        o_copy(s).wait_recv()

    def outer(s, finish):
        scale = weight_of(s) * tau
        rows = scale * edge
        mirrored = (-0.5 * scale) * 1.0
        mirror = recv_o[s]
        target = lax.rem(s + 1, 3)
        gathered = jnp.zeros((sector, radial), jnp.float32)
        for i in range(0, cells, CHUNK):
            at = pl.ds(i, CHUNK)
            q = [partial[n, :, at] for n in range(5)]
            ring = jnp.where(is_edge, recv_t[s, :, at], 0.0) * rows
            spun = [
                jnp.stack(
                    [
                        jnp.stack(
                            [
                                jnp.where(
                                    is_axis,
                                    mirrored * pltpu.roll(mirror, (radial - n * cells - i - k) % radial, 1),
                                    0.0,
                                )
                                for k in range(CHUNK)
                            ]
                        )
                        for n in (c, c + 1)
                    ]
                )
                for c in (0, 2)
            ]
            q[2] = q[2] + spun[0]
            q[3] = q[3] + ring[0:2]
            q[4] = q[4] + ring[2:4] + spun[1]
            for n in range(5):
                state[target, n, :, at] = q[n]
            if finish:
                pressure[:, pl.ds(cells + i, CHUNK)] = q[4]
            else:
                gathered = fluxes(s + 1, i, q, gathered)
        if not finish:
            send_o[s + 1] = gathered

    loads[0].wait()
    rho = flow[1]
    coef[0] = flow[0]
    coef[1] = rho
    coef[2] = rho * flow[2]
    coef[3] = 1.0 / rho
    loads[1].wait()
    gathered = jnp.zeros((sector, radial), jnp.float32)
    for i in range(0, cells, CHUNK):
        gathered = fluxes(0, i, [state[0, n, :, pl.ds(i, CHUNK)] for n in range(5)], gathered)
    send_o[0] = gathered

    pl.semaphore_wait(barrier, 3 + has_left.astype(jnp.int32) + has_right.astype(jnp.int32))
    send(0)

    loads[2].wait()
    loads[3].wait()
    loads[4].wait()

    def weigh(i, carry):
        length = width[i].astype(jnp.float32)
        inverse = 1.0 / (length * length)
        for shift in range(1, SEP + 1):
            weights[shift - 1, i] = jnp.exp(-(shift * shift) * inverse)
        return carry

    lax.fori_loop(0, cells, weigh, 0)

    def section(s, carry):
        inner(s)
        receive(s)
        outer(s, False)
        send(s + 1)
        return carry

    lax.fori_loop(0, SECTIONS - 1, section, 0)
    last = SECTIONS - 1
    inner(last)
    receive(last)
    outer(last, True)

    @pl.when(has_right)
    def _():
        p_copy(0).start()

    @pl.when(has_left)
    def _():
        p_copy(1).start()

    store = pltpu.make_async_copy(state.at[0], green, store_sem.at[0])
    store.start()

    @pl.when(has_left)
    def _():
        p_copy(0).wait_recv()

    @pl.when(has_right)
    def _():
        p_copy(1).wait_recv()

    def integrate(i, carry):
        re, im = pressure[0, cells + i], pressure[1, cells + i]
        sum_re, sum_im = re, im
        for shift in range(1, SEP + 1):
            w = weights[shift - 1, i]
            sum_re = sum_re + w * (pressure[0, cells + i + shift] + pressure[0, cells + i - shift])
            sum_im = sum_im + w * (pressure[1, cells + i + shift] + pressure[1, cells + i - shift])
        result[i] = amp[i] * (re * sum_re + im * sum_im)
        return carry

    lax.fori_loop(0, cells, integrate, 0)
    store_2 = pltpu.make_async_copy(result, intensity, store_sem.at[1])
    store_2.start()

    def drain(s, carry):
        o_copy(s).wait_send()
        t_copy(s, 0).wait_send()
        t_copy(s, 1).wait_send()

        @pl.when(has_right)
        def _():
            x_copy(s, 0).wait_send()

        @pl.when(has_left)
        def _():
            x_copy(s, 1).wait_send()

        return carry

    lax.fori_loop(0, SECTIONS, drain, 0)

    @pl.when(has_right)
    def _():
        p_copy(0).wait_send()

    @pl.when(has_left)
    def _():
        p_copy(1).wait_send()

    store.wait()
    store_2.wait()


def per_device(n_ax, n_az, adjoint, mean_flow, forcing, tke, half_width, start):
    cells, sector, radial = tke.shape
    block = (cells, sector, radial)
    f32 = jnp.float32
    any_spec = pl.BlockSpec(memory_space=pl.ANY)
    dma = pltpu.SemaphoreType.DMA
    vmem = lambda *shape: pltpu.VMEM(shape, f32)
    return pl.pallas_call(
        functools.partial(kernel, n_ax, n_az),
        out_shape=(
            jax.ShapeDtypeStruct(adjoint.shape, f32),
            jax.ShapeDtypeStruct(tke.shape, f32),
        ),
        in_specs=[pl.BlockSpec(memory_space=pltpu.SMEM)] + [any_spec] * 5,
        out_specs=(any_spec, any_spec),
        scratch_shapes=[
            vmem(3, 5, 2, *block),
            vmem(5, 2, *block),
            vmem(4, *block),
            vmem(2, *block),
            vmem(*block),
            vmem(*block),
            pltpu.VMEM(block, jnp.int32),
            vmem(SEP, *block),
            vmem(3, *block),
            vmem(*block),
            vmem(5, 2, cells + 2, sector, radial),
            vmem(SECTIONS, 6, *block),
            vmem(SECTIONS, 2, 5, 2, sector, radial),
            vmem(SECTIONS, 2, 5, 2, sector, radial),
            vmem(SECTIONS, 4, *block),
            vmem(SECTIONS, sector, radial),
            vmem(SECTIONS, sector, radial),
            vmem(2, 3 * cells, sector, radial),
            dma((5,)), dma((2,)),
            dma((SECTIONS, 2)), dma((SECTIONS, 2)),
            dma((SECTIONS, 2)), dma((SECTIONS, 2)),
            dma((SECTIONS,)), dma((SECTIONS,)),
            dma((2,)), dma((2,)),
        ],
        compiler_params=pltpu.CompilerParams(
            collective_id=0, has_side_effects=True, vmem_limit_bytes=60 * 2**20
        ),
    )(start, adjoint, mean_flow, forcing, tke, half_width)


def solution(mesh):
    return jax.shard_map(
        functools.partial(per_device, mesh.shape["ax"], mesh.shape["az"]),
        mesh=mesh,
        in_specs=(
            P(None, None, "ax", "az", None),
            P(None, "ax", "az", None),
            P(None, "ax", "az", None),
            P("ax", "az", None),
            P("ax", "az", None),
            P(),
        ),
        out_specs=(P(None, None, "ax", "az", None), P("ax", "az", None)),
        check_vma=False,
    )
```

```python
import functools
import math

import jax
import jax.numpy as jnp
from jax import lax
from jax.experimental import pallas as pl
from jax.experimental.pallas import tpu as pltpu
from jax.sharding import PartitionSpec as P

SEP = 16
SECTIONS = 6
ROUNDS = 3
NAXIAL = 2048
FREQUENCY = 0.7
MESH = pl.DeviceIdType.MESH
CHUNK = 4


def lane_pack(lane, gathered, value, to):
    moved = value if to == 0 else pltpu.roll(value, to, 1)
    return jnp.where(lane == to, moved, gathered)


def kernel(
    n_ax, n_az,
    start, adjoint, mean_flow, forcing, tke, half_width,
    green, intensity,
    state, partial, coef, force, sigma, amp, width, weights, flow, result,
    flux_x, flux_l, part_l, send_x, recv_x, recv_t, send_o, recv_o,
    send_d, recv_d, recv_a, send_p, recv_p, coef_x, coef_t, send_c, coef_o, pressure,
    load_sem, store_sem, x_send, x_recv, t_send, t_recv, o_send, o_recv, p_send, p_recv,
    d_send, d_recv, a_send, a_recv, b_send, b_recv, cx_send, cx_recv, ct_send, ct_recv, co_send, co_recv,
):
    cells, sector, radial = state.shape[3], state.shape[4], state.shape[5]
    ax, az = lax.axis_index("ax"), lax.axis_index("az")
    half_turn = n_az // 2
    left, right = ax - 1, ax + 1
    below, above = lax.rem(az + n_az - 1, n_az), lax.rem(az + 1, n_az)
    opposite = lax.rem(az + half_turn, n_az)
    opposite_below, opposite_above = lax.rem(az + half_turn - 1, n_az), lax.rem(az + half_turn + 1, n_az)
    has_left, has_right = ax > 0, ax < n_ax - 1
    sides = ((right, has_right), (left, has_left))
    turns = ((above, sector - 1, 0), (below, 0, sector - 1))

    loads = [
        pltpu.make_async_copy(src, dst, load_sem.at[n])
        for n, (src, dst) in enumerate(
            [(mean_flow, flow), (adjoint, state.at[0]), (forcing, force), (half_width, width), (tke, amp)]
        )
    ]
    for load in loads:
        load.start()

    barrier = pltpu.get_barrier_semaphore()

    def greet(i, k):
        pl.semaphore_signal(barrier, inc=1, device_id=(i, k), device_id_type=MESH)

    for i, there in sides:
        @pl.when(there)
        def _():
            for k in (opposite, below, above, az):
                greet(i, k)

    for k in (opposite_below, opposite_above, opposite, below, above):
        greet(ax, k)

    step_t = 2 * math.pi / (sector * n_az)
    lane = lax.broadcasted_iota(jnp.int32, (sector, radial), 1)
    row = lax.broadcasted_iota(jnp.int32, (sector, radial), 0)
    radius = lane.astype(jnp.float32) + 0.5
    tau = 0.8 / (2.0 + 1.0 / (radius * step_t))
    turn = 0.5 / (step_t * radius)
    outward = jnp.where(lane == radial - 1, 0.0, 0.5 * (radius + 1.0) / radius)
    inward = jnp.where(lane == 0, 0.0, 0.5 * (radius - 1.0) / radius)
    up = jnp.where(row == sector - 1, 0.0, turn)
    down = jnp.where(row == 0, 0.0, turn)
    is_edge = (row == 0) | (row == sector - 1)
    is_axis = lane == 0
    edge = jnp.where(row == 0, -turn, jnp.where(row == sector - 1, turn, 0.0))
    tau_0 = 0.8 / (2.0 + 1.0 / (0.5 * step_t))
    turn_0 = 0.5 / (step_t * 0.5)
    edge_0 = jnp.where(row == 0, -turn_0, jnp.where(row == sector - 1, turn_0, 0.0))

    first = start[0] + ax * cells
    pos = first + lax.broadcasted_iota(jnp.int32, (cells, sector, radial), 0)
    sigma[...] = 0.5 * (pos.astype(jnp.float32) + 0.5) / NAXIAL

    flux_x[:, :, 0] = jnp.zeros((5, 2, sector, radial), jnp.float32)
    flux_x[:, :, cells + 1] = jnp.zeros((5, 2, sector, radial), jnp.float32)

    @pl.when(jnp.logical_not(has_left))
    def _():
        pressure[:, 0:cells] = jnp.zeros((2, cells, sector, radial), jnp.float32)

    @pl.when(jnp.logical_not(has_right))
    def _():
        pressure[:, 2 * cells : 3 * cells] = jnp.zeros((2, cells, sector, radial), jnp.float32)

    def remote(src, dst, send_sem, recv_sem, i, k):
        return pltpu.make_async_remote_copy(
            src_ref=src, dst_ref=dst, send_sem=send_sem, recv_sem=recv_sem,
            device_id=(i, k), device_id_type=MESH,
        )

    def t_copy(r, later, way):
        who, mine, its = turns[way]
        source = part_l.at[r] if later else flux_l.at[2 * r, pl.ds(0, 4)]
        s = 2 * r + later
        return remote(
            source.at[:, :, mine], recv_t.at[s, :, :, its], t_send.at[s, way], t_recv.at[s, way], ax, who
        )

    def x_copy(s, way):
        return remote(send_x.at[s, way], recv_x.at[s, way], x_send.at[s, way], x_recv.at[s, way], sides[way][0], az)

    def o_copy(s):
        return remote(send_o.at[s], recv_o.at[s], o_send.at[s], o_recv.at[s], ax, opposite)

    def d_copy(r, way, spin):
        who, mine, its = turns[spin]
        return remote(
            send_d.at[r, way, :, mine], recv_d.at[r, way, :, its],
            d_send.at[r, way, spin], d_recv.at[r, way, spin], sides[way][0], who,
        )

    def a_copy(r, spin):
        _, mine, its = turns[spin]
        return remote(
            send_o.at[2 * r, pl.ds(mine, 1)], recv_a.at[r, pl.ds(its, 1)], a_send.at[r, spin], a_recv.at[r, spin],
            ax, (opposite_above, opposite_below)[spin],
        )

    def b_copy(r, way):
        return remote(
            send_p.at[r, way], recv_p.at[r, way], b_send.at[r, way], b_recv.at[r, way], sides[way][0], opposite
        )

    def cx_copy(way):
        return remote(
            coef.at[:, (cells - 1, 0)[way]], coef_x.at[way], cx_send.at[way], cx_recv.at[way], sides[way][0], az
        )

    def ct_copy(way):
        who, mine, its = turns[way]
        return remote(
            coef.at[pl.ds(1, 3), :, mine], coef_t.at[:, :, its], ct_send.at[way], ct_recv.at[way], ax, who
        )

    def co_copy():
        return remote(send_c, coef_o, co_send.at[0], co_recv.at[0], ax, opposite)

    def p_copy(way):
        return remote(
            pressure.at[:, pl.ds(cells, cells)], pressure.at[:, pl.ds((0, 2 * cells)[way], cells)],
            p_send.at[way], p_recv.at[way], sides[way][0], az,
        )

    def axial(q, u, rho, stiff, inv):
        a, b, c, d, e = q
        return (u * a, rho * a + stiff * e + u * b, u * c, u * d, b * inv + u * e)

    def fluxes(s, i, q, gathered):
        at = pl.ds(i, CHUNK)
        u, rho, stiff, inv = coef[0, at], coef[1, at], coef[2, at], coef[3, at]
        a, b, c, d, e = q
        shared = rho * a + stiff * e
        turned, spread = d * inv, c * inv
        along = (u * a, shared + u * b, u * c, u * d, b * inv + u * e)
        for n, f in enumerate(along):
            flux_x[n, :, pl.ds(i + 1, CHUNK)] = f
        flux_l[s, 0:2, at] = shared
        flux_l[s, 2:4, at] = turned
        flux_l[s, 4:6, at] = spread
        if gathered is None:
            return None
        r = s // 2
        for way, end, k in ((1, 0, 0), (0, cells - CHUNK, CHUNK - 1)):
            if i == end:
                for n, f in enumerate(along):
                    send_x[s, way, n] = f[:, k]
                for n, f in enumerate((along[0], along[3], along[4], shared, turned)):
                    send_d[r, way, 2 * n : 2 * n + 2] = f[:, k]
                packed = jnp.zeros((sector, radial), jnp.float32)
                for n, f in enumerate((shared, spread, along[0], along[2], along[4])):
                    for part in range(2):
                        packed = lane_pack(lane, packed, f[part, k], 2 * n + part)
                send_p[r, way] = packed
        for n, f in enumerate((shared, spread, turned)):
            for part in range(2):
                for k in range(CHUNK):
                    gathered[n] = lane_pack(lane, gathered[n], f[part, k], (2 * n + part) * cells + i + k)
        return gathered

    def nothing(count):
        return [jnp.zeros((sector, radial), jnp.float32) for _ in range(count)]

    def known(r):
        s = 2 * r + 1
        gathered = nothing(2)
        for i in range(0, cells, CHUNK):
            at = pl.ds(i, CHUNK)
            rho, stiff, inv = coef[1, at], coef[2, at], coef[3, at]
            shared = rho * partial[0, :, at] + stiff * partial[4, :, at]
            spread = partial[2, :, at] * inv
            part_l[r, 0:2, at] = shared
            part_l[r, 2:4, at] = partial[3, :, at] * inv
            for n, f in enumerate((shared, spread)):
                for part in range(2):
                    for k in range(CHUNK):
                        gathered[n] = lane_pack(lane, gathered[n], f[part, k], (2 * n + part) * cells + i + k)
        send_o[s] = jnp.where(lane < 2 * cells, gathered[0], gathered[1])
        o_copy(s).start()
        t_copy(r, 1, 0).start()
        t_copy(r, 1, 1).start()
        for way, i in ((1, 0), (0, cells - 1)):
            q = [partial[n, :, i] for n in range(5)]
            for n, f in enumerate(axial(q, coef[0, i], coef[1, i], coef[2, i], coef[3, i])):
                send_x[s, way, n] = f
        for way in range(2):
            @pl.when(sides[way][1])
            def _():
                x_copy(s, way).start()

    def send(r):
        for way in range(2):
            @pl.when(sides[way][1])
            def _():
                b_copy(r, way).start()

        a_copy(r, 0).start()
        a_copy(r, 1).start()
        o_copy(2 * r).start()
        for way in range(2):
            @pl.when(sides[way][1])
            def _():
                d_copy(r, way, 0).start()
                d_copy(r, way, 1).start()

        t_copy(r, 0, 0).start()
        t_copy(r, 0, 1).start()
        for way in range(2):
            @pl.when(sides[way][1])
            def _():
                x_copy(2 * r, way).start()

    def weight_of(s):
        third = lax.rem(s, 3)
        return jnp.where(third == 0, 1.0 / 3.0, jnp.where(third == 1, 0.5, 1.0))

    def inner(s):
        source = lax.rem(s, 3)
        scale = weight_of(s) * tau

        def body(t, carry):
            i = t * CHUNK
            at = pl.ds(i, CHUNK)
            damp = sigma[at]
            shared, turned, spread = flux_l[s, 0:2, at], flux_l[s, 2:4, at], flux_l[s, 4:6, at]

            def radially(f):
                return outward * pltpu.roll(f, radial - 1, 3) - inward * pltpu.roll(f, 1, 3)

            def around(f):
                return up * pltpu.roll(f, sector - 1, 2) - down * pltpu.roll(f, 1, 2)

            extra = (None, None, radially(shared), around(shared), radially(spread) + around(turned) + force[:, at])
            for n in range(5):
                q = state[source, n, :, at]
                total = 0.5 * (flux_x[n, :, pl.ds(i + 2, CHUNK)] - flux_x[n, :, at]) - damp * q
                if extra[n] is not None:
                    total = total + extra[n]
                base = state[0, n, :, at]
                partial[n, 0, at] = base[0] + scale * (total[0] + FREQUENCY * q[1])
                partial[n, 1, at] = base[1] + scale * (total[1] - FREQUENCY * q[0])
            return carry

        lax.fori_loop(0, cells // CHUNK, body, 0)

    def receive(r, later):
        s = 2 * r + later
        for way in range(2):
            @pl.when(sides[1 - way][1])
            def _():
                x_copy(s, way).wait_recv()

        t_copy(r, later, 0).wait_recv()
        t_copy(r, later, 1).wait_recv()
        o_copy(s).wait_recv()

    def complete(r):
        s = 2 * r + 1
        scale = weight_of(2 * r) * tau
        half = 0.5 * scale
        scale_0 = weight_of(2 * r) * tau_0
        half_0 = 0.5 * scale_0
        around = scale * edge
        a_copy(r, 0).wait_recv()
        a_copy(r, 1).wait_recv()
        aside = jnp.where(is_edge, recv_a[r], 0.0)
        axis = -half_0 * aside

        for i in range(0, cells, CHUNK):
            at = pl.ds(i, CHUNK)
            spun = jnp.stack(
                [
                    jnp.stack(
                        [
                            jnp.where(is_axis, pltpu.roll(axis, radial - (2 + part) * cells - i - k, 1), 0.0)
                            for k in range(CHUNK)
                        ]
                    )
                    for part in range(2)
                ]
            )
            more_d = -around * flux_l[2 * r, 0:2, at]
            more_e = spun - around * flux_l[2 * r, 2:4, at]
            recv_t[s, 0:2, at] = recv_t[s, 0:2, at] + coef_t[1, at] * more_e
            recv_t[s, 2:4, at] = recv_t[s, 2:4, at] + coef_t[2, at] * more_d

        mine = send_o[2 * r]
        more_c = -half_0 * pltpu.roll(mine, 2 * cells, 1)
        more_e = -half_0 * pltpu.roll(mine, radial - 2 * cells, 1) + scale_0 * edge_0 * pltpu.roll(
            aside, radial - 4 * cells, 1
        )
        recv_o[s] = (
            recv_o[s]
            + coef_o[0] * jnp.where(lane < 2 * cells, 0.0, more_c)
            + coef_o[1] * jnp.where(lane < 2 * cells, more_e, 0.0)
        )

        for way, i, sign in ((0, 0, 1.0), (1, cells - 1, -1.0)):
            @pl.when(sides[1 - way][1])
            def _():
                d_copy(r, way, 0).wait_recv()
                d_copy(r, way, 1).wait_recv()
                corner = jnp.where(is_edge, recv_d[r, way], 0.0)
                gone = (-sign * half) * corner[0:6]
                recv_t[s, 0:2, i] = recv_t[s, 0:2, i] + coef_t[0, i] * gone[0:2] + coef_t[1, i] * gone[4:6]
                recv_t[s, 2:4, i] = recv_t[s, 2:4, i] + coef_t[2, i] * gone[2:4]
                b_copy(r, way).wait_recv()
                packed = recv_p[r, way]

                def at_axis(n):
                    return jnp.stack(
                        [
                            jnp.where(is_axis, packed if n + part == 0 else pltpu.roll(packed, radial - n - part, 1), 0.0)
                            for part in range(2)
                        ]
                    )

                more = [(sign * half) * send_x[2 * r, 1 - way, n] for n in range(5)]
                more[2] = more[2] - half * at_axis(0)
                more[3] = more[3] + around * corner[6:8]
                more[4] = more[4] + around * corner[8:10] - half * at_axis(2)
                c = coef_x[way]
                for n, f in enumerate(axial(more, c[0], c[1], c[2], c[3])):
                    recv_x[s, way, n] = recv_x[s, way, n] + f

                def spread_out(n, to):
                    low = pltpu.roll(packed, (radial + to + i - n) % radial, 1)
                    high = pltpu.roll(packed, (radial + to + cells + i - n - 1) % radial, 1)
                    return jnp.where(lane == to + i, low, jnp.where(lane == to + cells + i, high, 0.0))

                recv_o[s] = recv_o[s] - (sign * half_0) * (
                    coef_o[0] * (spread_out(4, 0) + spread_out(6, 2 * cells)) + coef_o[1] * spread_out(8, 0)
                )

    def outer(s, then):
        scale = weight_of(s) * tau
        half = 0.5 * scale
        for way, i, sign in ((0, 0, -1.0), (1, cells - 1, 1.0)):
            @pl.when(sides[1 - way][1])
            def _():
                partial[:, :, i] = partial[:, :, i] + (sign * half) * recv_x[s, way]

        rows = scale * edge
        mirror = (-0.5 * tau_0) * weight_of(s) * recv_o[s]
        target = lax.rem(s + 1, 3)
        gathered = nothing(3) if then == "round" else None
        for i in range(0, cells, CHUNK):
            at = pl.ds(i, CHUNK)
            q = [partial[n, :, at] for n in range(5)]
            ring = jnp.where(is_edge, recv_t[s, :, at], 0.0) * rows
            spun = [
                jnp.stack(
                    [
                        jnp.stack(
                            [
                                jnp.where(is_axis, pltpu.roll(mirror, (radial - n * cells - i - k) % radial, 1), 0.0)
                                for k in range(CHUNK)
                            ]
                        )
                        for n in (c, c + 1)
                    ]
                )
                for c in (0, 2)
            ]
            q[2] = q[2] + spun[0]
            q[3] = q[3] + ring[0:2]
            q[4] = q[4] + ring[2:4] + spun[1]
            for n in range(5):
                state[target, n, :, at] = q[n]
            if then == "none":
                pressure[:, pl.ds(cells + i, CHUNK)] = q[4]
            else:
                gathered = fluxes(s + 1, i, q, gathered)
        if then == "round":
            join(s + 1, gathered)

    def join(s, gathered):
        send_o[s] = jnp.where(lane < 2 * cells, gathered[0], jnp.where(lane < 4 * cells, gathered[1], gathered[2]))

    loads[0].wait()
    rho = flow[1]
    coef[0] = flow[0]
    coef[1] = rho
    coef[2] = rho * flow[2]
    coef[3] = 1.0 / rho
    loads[1].wait()
    gathered = nothing(3)
    for i in range(0, cells, CHUNK):
        gathered = fluxes(0, i, [state[0, n, :, pl.ds(i, CHUNK)] for n in range(5)], gathered)
    join(0, gathered)

    there = has_left.astype(jnp.int32) + has_right.astype(jnp.int32)
    pl.semaphore_wait(barrier, 5 + 4 * there)
    send(0)

    gathered = nothing(3)
    for n, which in enumerate((1, 3, 2)):
        for i in range(cells):
            gathered[n] = lane_pack(lane, gathered[n], coef[which, i], (0, 2, 0)[n] * cells + i)
    wide = [jnp.where(lane % (2 * cells) < cells, g, pltpu.roll(g, cells, 1)) for g in gathered]
    send_c[0] = jnp.where(lane < 2 * cells, wide[0], jnp.where(lane < 4 * cells, wide[1], 0.0))
    send_c[1] = jnp.where(lane < 2 * cells, wide[2], 0.0)
    co_copy().start()
    ct_copy(0).start()
    ct_copy(1).start()
    for way in range(2):
        @pl.when(sides[way][1])
        def _():
            cx_copy(way).start()

    loads[2].wait()

    def first_half(r):
        inner(2 * r)
        known(r)
        receive(r, 0)
        outer(2 * r, "plain")
        inner(2 * r + 1)
        receive(r, 1)

    def round_(r, carry):
        first_half(r)

        @pl.when(r == 0)
        def _():
            co_copy().wait_recv()
            ct_copy(0).wait_recv()
            ct_copy(1).wait_recv()
            for way in range(2):
                @pl.when(sides[1 - way][1])
                def _():
                    cx_copy(way).wait_recv()

        complete(r)
        outer(2 * r + 1, "round")
        send(r + 1)

        @pl.when(r == 0)
        def _():
            loads[3].wait()

            def weigh(i, carry):
                length = width[i].astype(jnp.float32)
                inverse = 1.0 / (length * length)
                for shift in range(1, SEP + 1):
                    weights[shift - 1, i] = jnp.exp(-(shift * shift) * inverse)
                return carry

            lax.fori_loop(0, cells, weigh, 0)

        return carry

    lax.fori_loop(0, ROUNDS - 1, round_, 0)
    last = ROUNDS - 1
    first_half(last)
    complete(last)
    outer(2 * last + 1, "none")

    for way in range(2):
        @pl.when(sides[way][1])
        def _():
            p_copy(way).start()

    store = pltpu.make_async_copy(state.at[0], green, store_sem.at[0])
    store.start()
    loads[4].wait()
    for way in range(2):
        @pl.when(sides[1 - way][1])
        def _():
            p_copy(way).wait_recv()

    def integrate(i, carry):
        re, im = pressure[0, cells + i], pressure[1, cells + i]
        sum_re, sum_im = re, im
        for shift in range(1, SEP + 1):
            w = weights[shift - 1, i]
            sum_re = sum_re + w * (pressure[0, cells + i + shift] + pressure[0, cells + i - shift])
            sum_im = sum_im + w * (pressure[1, cells + i + shift] + pressure[1, cells + i - shift])
        result[i] = amp[i] * (re * sum_re + im * sum_im)
        return carry

    lax.fori_loop(0, cells, integrate, 0)
    store_2 = pltpu.make_async_copy(result, intensity, store_sem.at[1])
    store_2.start()

    def drain(r, carry):
        for s in (2 * r, 2 * r + 1):
            o_copy(s).wait_send()
            for way in range(2):
                @pl.when(sides[way][1])
                def _():
                    x_copy(s, way).wait_send()

        for way in range(2):
            t_copy(r, 0, way).wait_send()
            t_copy(r, 1, way).wait_send()
            a_copy(r, way).wait_send()

            @pl.when(sides[way][1])
            def _():
                b_copy(r, way).wait_send()
                d_copy(r, way, 0).wait_send()
                d_copy(r, way, 1).wait_send()

        return carry

    lax.fori_loop(0, ROUNDS, drain, 0)
    co_copy().wait_send()
    for way in range(2):
        ct_copy(way).wait_send()

        @pl.when(sides[way][1])
        def _():
            cx_copy(way).wait_send()
            p_copy(way).wait_send()

    store.wait()
    store_2.wait()


def per_device(n_ax, n_az, adjoint, mean_flow, forcing, tke, half_width, start):
    cells, sector, radial = tke.shape
    block = (cells, sector, radial)
    tile = (sector, radial)
    f32 = jnp.float32
    any_spec = pl.BlockSpec(memory_space=pl.ANY)

    def dma(*shape):
        return pltpu.SemaphoreType.DMA(shape)

    def vmem(*shape):
        return pltpu.VMEM(shape, f32)

    return pl.pallas_call(
        functools.partial(kernel, n_ax, n_az),
        out_shape=(
            jax.ShapeDtypeStruct(adjoint.shape, f32),
            jax.ShapeDtypeStruct(tke.shape, f32),
        ),
        in_specs=[pl.BlockSpec(memory_space=pltpu.SMEM)] + [any_spec] * 5,
        out_specs=(any_spec, any_spec),
        scratch_shapes=[
            vmem(3, 5, 2, *block),
            vmem(5, 2, *block),
            vmem(4, *block),
            vmem(2, *block),
            vmem(*block),
            vmem(*block),
            pltpu.VMEM(block, jnp.int32),
            vmem(SEP, *block),
            vmem(3, *block),
            vmem(*block),
            vmem(5, 2, cells + 2, *tile),
            vmem(SECTIONS, 6, *block),
            vmem(ROUNDS, 4, *block),
            vmem(SECTIONS, 2, 5, 2, *tile),
            vmem(SECTIONS, 2, 5, 2, *tile),
            vmem(SECTIONS, 4, *block),
            vmem(SECTIONS, *tile),
            vmem(SECTIONS, *tile),
            vmem(ROUNDS, 2, 10, *tile),
            vmem(ROUNDS, 2, 10, *tile),
            vmem(ROUNDS, *tile),
            vmem(ROUNDS, 2, *tile),
            vmem(ROUNDS, 2, *tile),
            vmem(2, 4, *tile),
            vmem(3, *block),
            vmem(2, *tile),
            vmem(2, *tile),
            vmem(2, 3 * cells, *tile),
            dma(5), dma(2),
            dma(SECTIONS, 2), dma(SECTIONS, 2),
            dma(SECTIONS, 2), dma(SECTIONS, 2),
            dma(SECTIONS), dma(SECTIONS),
            dma(2), dma(2),
            dma(ROUNDS, 2, 2), dma(ROUNDS, 2, 2),
            dma(ROUNDS, 2), dma(ROUNDS, 2),
            dma(ROUNDS, 2), dma(ROUNDS, 2),
            dma(2), dma(2),
            dma(2), dma(2),
            dma(1), dma(1),
        ],
        compiler_params=pltpu.CompilerParams(
            collective_id=0, has_side_effects=True, vmem_limit_bytes=60 * 2**20
        ),
    )(start, adjoint, mean_flow, forcing, tke, half_width)


def solution(mesh):
    return jax.shard_map(
        functools.partial(per_device, mesh.shape["ax"], mesh.shape["az"]),
        mesh=mesh,
        in_specs=(
            P(None, None, "ax", "az", None),
            P(None, "ax", "az", None),
            P(None, "ax", "az", None),
            P("ax", "az", None),
            P("ax", "az", None),
            P(),
        ),
        out_specs=(P(None, None, "ax", "az", None), P("ax", "az", None)),
        check_vma=False,
    )
```

```python
import functools
import math

import jax
import jax.numpy as jnp
from jax import lax
from jax.experimental import pallas as pl
from jax.experimental.pallas import tpu as pltpu
from jax.sharding import PartitionSpec as P

SEP = 16
SECTIONS = 6
ROUNDS = 3
NAXIAL = 2048
FREQUENCY = 0.7
MESH = pl.DeviceIdType.MESH
CHUNK = 4


def lane_pack(lane, gathered, value, to):
    moved = value if to == 0 else pltpu.roll(value, to, 1)
    return jnp.where(lane == to, moved, gathered)


def kernel(
    n_ax, n_az,
    start, adjoint, mean_flow, forcing, tke, half_width,
    green, intensity,
    state, partial, coef, force, sigma, amp, width, weights, flow, result,
    flux_x, flux_l, part_l, send_x, recv_x, recv_t, send_o, recv_o,
    send_d, recv_d, recv_a, extra_o, send_p, recv_p, coef_x, coef_t, send_c, coef_o, pressure,
    load_sem, store_sem, x_send, x_recv, t_send, t_recv, o_send, o_recv, p_send, p_recv,
    d_send, d_recv, a_send, a_recv, b_send, b_recv, cx_send, cx_recv, ct_send, ct_recv, co_send, co_recv,
):
    cells, sector, radial = state.shape[3], state.shape[4], state.shape[5]
    ax, az = lax.axis_index("ax"), lax.axis_index("az")
    half_turn = n_az // 2
    left, right = ax - 1, ax + 1
    below, above = lax.rem(az + n_az - 1, n_az), lax.rem(az + 1, n_az)
    opposite = lax.rem(az + half_turn, n_az)
    opposite_below, opposite_above = lax.rem(az + half_turn - 1, n_az), lax.rem(az + half_turn + 1, n_az)
    has_left, has_right = ax > 0, ax < n_ax - 1
    sides = ((right, has_right), (left, has_left))
    turns = ((above, sector - 1, 0), (below, 0, sector - 1))

    loads = [
        pltpu.make_async_copy(src, dst, load_sem.at[n])
        for n, (src, dst) in enumerate(
            [(mean_flow, flow), (adjoint, state.at[0]), (forcing, force), (half_width, width), (tke, amp)]
        )
    ]
    for load in loads:
        load.start()

    barrier = pltpu.get_barrier_semaphore()

    def greet(i, k):
        pl.semaphore_signal(barrier, inc=1, device_id=(i, k), device_id_type=MESH)

    for i, there in sides:
        @pl.when(there)
        def _():
            for k in (opposite, below, above, az):
                greet(i, k)

    for k in (opposite_below, opposite_above, opposite, below, above):
        greet(ax, k)

    step_t = 2 * math.pi / (sector * n_az)
    lane = lax.broadcasted_iota(jnp.int32, (sector, radial), 1)
    row = lax.broadcasted_iota(jnp.int32, (sector, radial), 0)
    radius = lane.astype(jnp.float32) + 0.5
    tau = 0.8 / (2.0 + 1.0 / (radius * step_t))
    turn = 0.5 / (step_t * radius)
    outward = jnp.where(lane == radial - 1, 0.0, 0.5 * (radius + 1.0) / radius)
    inward = jnp.where(lane == 0, 0.0, 0.5 * (radius - 1.0) / radius)
    up = jnp.where(row == sector - 1, 0.0, turn)
    down = jnp.where(row == 0, 0.0, turn)
    is_edge = (row == 0) | (row == sector - 1)
    is_axis = lane == 0
    edge = jnp.where(row == 0, -turn, jnp.where(row == sector - 1, turn, 0.0))
    tau_0 = 0.8 / (2.0 + 1.0 / (0.5 * step_t))
    turn_0 = 0.5 / (step_t * 0.5)
    edge_0 = jnp.where(row == 0, -turn_0, jnp.where(row == sector - 1, turn_0, 0.0))

    first = start[0] + ax * cells
    pos = first + lax.broadcasted_iota(jnp.int32, (cells, sector, radial), 0)
    sigma[...] = 0.5 * (pos.astype(jnp.float32) + 0.5) / NAXIAL

    flux_x[:, :, 0] = jnp.zeros((5, 2, sector, radial), jnp.float32)
    flux_x[:, :, cells + 1] = jnp.zeros((5, 2, sector, radial), jnp.float32)

    @pl.when(jnp.logical_not(has_left))
    def _():
        pressure[:, 0:cells] = jnp.zeros((2, cells, sector, radial), jnp.float32)

    @pl.when(jnp.logical_not(has_right))
    def _():
        pressure[:, 2 * cells : 3 * cells] = jnp.zeros((2, cells, sector, radial), jnp.float32)

    def remote(src, dst, send_sem, recv_sem, i, k):
        return pltpu.make_async_remote_copy(
            src_ref=src, dst_ref=dst, send_sem=send_sem, recv_sem=recv_sem,
            device_id=(i, k), device_id_type=MESH,
        )

    def t_copy(r, later, way):
        who, mine, its = turns[way]
        source = part_l.at[r] if later else flux_l.at[2 * r, pl.ds(0, 4)]
        s = 2 * r + later
        return remote(
            source.at[:, :, mine], recv_t.at[s, :, :, its], t_send.at[s, way], t_recv.at[s, way], ax, who
        )

    def x_copy(s, way):
        return remote(send_x.at[s, way], recv_x.at[s, way], x_send.at[s, way], x_recv.at[s, way], sides[way][0], az)

    def o_copy(s):
        return remote(send_o.at[s], recv_o.at[s], o_send.at[s], o_recv.at[s], ax, opposite)

    def d_copy(r, way, spin):
        who, mine, its = turns[spin]
        return remote(
            send_d.at[r, way, :, mine], recv_d.at[r, way, :, its],
            d_send.at[r, way, spin], d_recv.at[r, way, spin], sides[way][0], who,
        )

    def a_copy(r, spin):
        _, mine, its = turns[spin]
        return remote(
            send_o.at[2 * r, pl.ds(mine, 1)], recv_a.at[r, pl.ds(its, 1)], a_send.at[r, spin], a_recv.at[r, spin],
            ax, (opposite_above, opposite_below)[spin],
        )

    def b_copy(r, way):
        return remote(
            send_p.at[r, way], recv_p.at[r, way], b_send.at[r, way], b_recv.at[r, way], sides[way][0], opposite
        )

    def cx_copy(way):
        return remote(
            coef.at[:, (cells - 1, 0)[way]], coef_x.at[way], cx_send.at[way], cx_recv.at[way], sides[way][0], az
        )

    def ct_copy(way):
        who, mine, its = turns[way]
        return remote(
            coef.at[pl.ds(1, 3), :, mine], coef_t.at[:, :, its], ct_send.at[way], ct_recv.at[way], ax, who
        )

    def co_copy():
        return remote(send_c, coef_o, co_send.at[0], co_recv.at[0], ax, opposite)

    def p_copy(way, piece):
        first, count = ((1, cells - 2), (0, 1), (cells - 1, 1))[piece]
        return remote(
            pressure.at[:, pl.ds(cells + first, count)],
            pressure.at[:, pl.ds((0, 2 * cells)[way] + first, count)],
            p_send.at[way, piece], p_recv.at[way, piece], sides[way][0], az,
        )

    def axial(q, u, rho, stiff, inv):
        a, b, c, d, e = q
        return (u * a, rho * a + stiff * e + u * b, u * c, u * d, b * inv + u * e)

    def fluxes(s, i, q, gathered):
        count = q[0].shape[1]
        at = pl.ds(i, count)
        u, rho, stiff, inv = coef[0, at], coef[1, at], coef[2, at], coef[3, at]
        a, b, c, d, e = q
        shared = rho * a + stiff * e
        turned, spread = d * inv, c * inv
        along = (u * a, shared + u * b, u * c, u * d, b * inv + u * e)
        for n, f in enumerate(along):
            flux_x[n, :, pl.ds(i + 1, count)] = f
        flux_l[s, 0:2, at] = shared
        flux_l[s, 2:4, at] = turned
        flux_l[s, 4:6, at] = spread
        if gathered is None:
            return None
        r = s // 2
        for way, k in ((1, -i), (0, cells - 1 - i)):
            if 0 <= k < count:
                for n, f in enumerate(along):
                    send_x[s, way, n] = f[:, k]
                for n, f in enumerate((along[0], along[3], along[4], shared, turned)):
                    send_d[r, way, 2 * n : 2 * n + 2] = f[:, k]
                packed = jnp.zeros((sector, radial), jnp.float32)
                for n, f in enumerate((shared, spread, along[0], along[2], along[4])):
                    for part in range(2):
                        packed = lane_pack(lane, packed, f[part, k], 2 * n + part)
                send_p[r, way] = packed
        for n, f in enumerate((shared, spread, turned)):
            for part in range(2):
                for k in range(count):
                    gathered[n] = lane_pack(lane, gathered[n], f[part, k], (2 * n + part) * cells + i + k)
        return gathered

    def nothing(count):
        return [jnp.zeros((sector, radial), jnp.float32) for _ in range(count)]

    def known(r):
        s = 2 * r + 1
        gathered = nothing(2)
        for i in range(0, cells, CHUNK):
            at = pl.ds(i, CHUNK)
            rho, stiff, inv = coef[1, at], coef[2, at], coef[3, at]
            shared = rho * partial[0, :, at] + stiff * partial[4, :, at]
            spread = partial[2, :, at] * inv
            part_l[r, 0:2, at] = shared
            part_l[r, 2:4, at] = partial[3, :, at] * inv
            for n, f in enumerate((shared, spread)):
                for part in range(2):
                    for k in range(CHUNK):
                        gathered[n] = lane_pack(lane, gathered[n], f[part, k], (2 * n + part) * cells + i + k)
        send_o[s] = jnp.where(lane < 2 * cells, gathered[0], gathered[1])
        o_copy(s).start()
        t_copy(r, 1, 0).start()
        t_copy(r, 1, 1).start()
        for way, i in ((1, 0), (0, cells - 1)):
            q = [partial[n, :, i] for n in range(5)]
            for n, f in enumerate(axial(q, coef[0, i], coef[1, i], coef[2, i], coef[3, i])):
                send_x[s, way, n] = f
        for way in range(2):
            @pl.when(sides[way][1])
            def _():
                x_copy(s, way).start()

    def send(r):
        for way in range(2):
            @pl.when(sides[way][1])
            def _():
                b_copy(r, way).start()

        a_copy(r, 0).start()
        a_copy(r, 1).start()
        o_copy(2 * r).start()
        for way in range(2):
            @pl.when(sides[way][1])
            def _():
                d_copy(r, way, 0).start()
                d_copy(r, way, 1).start()

        t_copy(r, 0, 0).start()
        t_copy(r, 0, 1).start()
        for way in range(2):
            @pl.when(sides[way][1])
            def _():
                x_copy(2 * r, way).start()

    def weight_of(s):
        third = lax.rem(s, 3)
        return jnp.where(third == 0, 1.0 / 3.0, jnp.where(third == 1, 0.5, 1.0))

    def inner(s):
        source = lax.rem(s, 3)
        scale = weight_of(s) * tau

        half = 0.5 * scale
        turned_by = scale * FREQUENCY

        def radially(f):
            return outward * pltpu.roll(f, radial - 1, 3) - inward * pltpu.roll(f, 1, 3)

        def around(f):
            return up * pltpu.roll(f, sector - 1, 2) - down * pltpu.roll(f, 1, 2)

        for i in range(0, cells, CHUNK):
            at = pl.ds(i, CHUNK)
            fade = scale * sigma[at]
            shared, turned, spread = flux_l[s, 0:2, at], flux_l[s, 2:4, at], flux_l[s, 4:6, at]
            extra = (None, None, radially(shared), around(shared), radially(spread) + around(turned) + force[:, at])
            for n in range(5):
                q = state[source, n, :, at]
                total = state[0, n, :, at] + half * (flux_x[n, :, pl.ds(i + 2, CHUNK)] - flux_x[n, :, at]) - fade * q
                if extra[n] is not None:
                    total = total + scale * extra[n]
                partial[n, 0, at] = total[0] + turned_by * q[1]
                partial[n, 1, at] = total[1] - turned_by * q[0]

    def receive(r, later):
        s = 2 * r + later
        for way in range(2):
            @pl.when(sides[1 - way][1])
            def _():
                x_copy(s, way).wait_recv()

        t_copy(r, later, 0).wait_recv()
        t_copy(r, later, 1).wait_recv()
        o_copy(s).wait_recv()

    def complete(r):
        scale, scale_0 = weight_of(2 * r) * tau, weight_of(2 * r) * tau_0
        half, half_0 = 0.5 * scale, 0.5 * scale_0
        around = scale * edge
        scale_2 = weight_of(2 * r + 1) * tau
        rows = scale_2 * edge
        a_copy(r, 0).wait_recv()
        a_copy(r, 1).wait_recv()
        aside = jnp.where(is_edge, recv_a[r], 0.0)
        axis = -half_0 * aside

        for i in range(0, cells, CHUNK):
            at = pl.ds(i, CHUNK)
            spun = jnp.stack(
                [
                    jnp.stack(
                        [
                            jnp.where(is_axis, pltpu.roll(axis, radial - (2 + part) * cells - i - k, 1), 0.0)
                            for k in range(CHUNK)
                        ]
                    )
                    for part in range(2)
                ]
            )
            more_d = -around * flux_l[2 * r, 0:2, at]
            more_e = spun - around * flux_l[2 * r, 2:4, at]
            partial[3, :, at] = partial[3, :, at] + rows * jnp.where(is_edge, coef_t[1, at] * more_e, 0.0)
            partial[4, :, at] = partial[4, :, at] + rows * jnp.where(is_edge, coef_t[2, at] * more_d, 0.0)

        mine = send_o[2 * r]
        more_c = -half_0 * pltpu.roll(mine, 2 * cells, 1)
        more_e = -half_0 * pltpu.roll(mine, radial - 2 * cells, 1) + scale_0 * edge_0 * pltpu.roll(
            aside, radial - 4 * cells, 1
        )
        extra_o[...] = coef_o[0] * jnp.where(lane < 2 * cells, 0.0, more_c) + coef_o[1] * jnp.where(
            lane < 2 * cells, more_e, 0.0
        )

        for way, i, sign in ((0, 0, 1.0), (1, cells - 1, -1.0)):
            @pl.when(sides[1 - way][1])
            def _():
                d_copy(r, way, 0).wait_recv()
                d_copy(r, way, 1).wait_recv()
                corner = jnp.where(is_edge, recv_d[r, way], 0.0)
                gone = (-sign * half) * corner[0:6]
                more = [(sign * half) * send_x[2 * r, 1 - way, n] for n in range(5)]
                more[3] = more[3] + around * corner[6:8]
                more[4] = more[4] + around * corner[8:10]
                c = coef_x[way]
                along = axial(more, c[0], c[1], c[2], c[3])
                turned = [None, None, None]
                turned += [rows * jnp.where(is_edge, coef_t[0, i] * gone[0:2] + coef_t[1, i] * gone[4:6], 0.0)]
                turned += [rows * jnp.where(is_edge, coef_t[2, i] * gone[2:4], 0.0)]
                for n in range(5):
                    q = partial[n, :, i] - (0.5 * sign * scale_2) * along[n]
                    partial[n, :, i] = q if turned[n] is None else q + turned[n]

    def complete_ends(r):
        half_0 = (0.5 * tau_0) * weight_of(2 * r)
        half = (0.5 * weight_of(2 * r + 1)) * tau
        for way, i, sign in ((0, 0, 1.0), (1, cells - 1, -1.0)):
            @pl.when(sides[1 - way][1])
            def _():
                b_copy(r, way).wait_recv()
                packed = -half_0 * recv_p[r, way]

                def at_axis(n):
                    return jnp.stack(
                        [
                            jnp.where(is_axis, packed if n + part == 0 else pltpu.roll(packed, radial - n - part, 1), 0.0)
                            for part in range(2)
                        ]
                    )

                c, e = (-sign * half) * at_axis(0), (-sign * half) * at_axis(2)
                u, stiff = coef_x[way, 0], coef_x[way, 2]
                partial[1, :, i] = partial[1, :, i] + stiff * e
                partial[2, :, i] = partial[2, :, i] + u * c
                partial[4, :, i] = partial[4, :, i] + u * e

                def spread_out(n, to):
                    low = pltpu.roll(packed, (radial + to + i - n) % radial, 1)
                    high = pltpu.roll(packed, (radial + to + cells + i - n - 1) % radial, 1)
                    return jnp.where(lane == to + i, low, jnp.where(lane == to + cells + i, high, 0.0))

                extra_o[...] = extra_o[...] + sign * (
                    coef_o[0] * (spread_out(4, 0) + spread_out(6, 2 * cells)) + coef_o[1] * spread_out(8, 0)
                )

    def add_x(s):
        half = (0.5 * weight_of(s)) * tau
        for way, i, sign in ((0, 0, -1.0), (1, cells - 1, 1.0)):
            @pl.when(sides[1 - way][1])
            def _():
                partial[:, :, i] = partial[:, :, i] + (sign * half) * recv_x[s, way]

    def outer(s, chunks, then, gathered=None):
        scale = weight_of(s) * tau
        rows = scale * edge
        mirror = recv_o[s] if then == "plain" else recv_o[s] + extra_o[...]
        mirror = (-0.5 * tau_0) * weight_of(s) * mirror
        target = lax.rem(s + 1, 3)
        for i, count in chunks:
            at = pl.ds(i, count)
            q = [partial[n, :, at] for n in range(5)]
            ring = jnp.where(is_edge, recv_t[s, :, at], 0.0) * rows
            spun = [
                jnp.stack(
                    [
                        jnp.stack(
                            [
                                jnp.where(is_axis, pltpu.roll(mirror, (radial - n * cells - i - k) % radial, 1), 0.0)
                                for k in range(count)
                            ]
                        )
                        for n in (c, c + 1)
                    ]
                )
                for c in (0, 2)
            ]
            q[2] = q[2] + spun[0]
            q[3] = q[3] + ring[0:2]
            q[4] = q[4] + ring[2:4] + spun[1]
            for n in range(5):
                state[target, n, :, at] = q[n]
            if then == "none":
                pressure[:, pl.ds(cells + i, count)] = q[4]
            else:
                gathered = fluxes(s + 1, i, q, gathered)
        return gathered

    def join(s, gathered):
        send_o[s] = jnp.where(lane < 2 * cells, gathered[0], jnp.where(lane < 4 * cells, gathered[1], gathered[2]))

    loads[0].wait()
    rho = flow[1]
    coef[0] = flow[0]
    coef[1] = rho
    coef[2] = rho * flow[2]
    coef[3] = 1.0 / rho
    loads[1].wait()
    gathered = nothing(3)
    for i in range(0, cells, CHUNK):
        gathered = fluxes(0, i, [state[0, n, :, pl.ds(i, CHUNK)] for n in range(5)], gathered)
    join(0, gathered)

    there = has_left.astype(jnp.int32) + has_right.astype(jnp.int32)
    pl.semaphore_wait(barrier, 5 + 4 * there)
    send(0)

    gathered = nothing(3)
    for n, which in enumerate((1, 3, 2)):
        for i in range(cells):
            gathered[n] = lane_pack(lane, gathered[n], coef[which, i], (0, 2, 0)[n] * cells + i)
    wide = [jnp.where(lane % (2 * cells) < cells, g, pltpu.roll(g, cells, 1)) for g in gathered]
    send_c[0] = jnp.where(lane < 2 * cells, wide[0], jnp.where(lane < 4 * cells, wide[1], 0.0))
    send_c[1] = jnp.where(lane < 2 * cells, wide[2], 0.0)
    co_copy().start()
    ct_copy(0).start()
    ct_copy(1).start()
    for way in range(2):
        @pl.when(sides[way][1])
        def _():
            cx_copy(way).start()

    loads[2].wait()
    whole = [(i, CHUNK) for i in range(0, cells, CHUNK)]
    middle = [(i, min(CHUNK, cells - 1 - i)) for i in range(1, cells - 1, CHUNK)]
    ends = [(0, 1), (cells - 1, 1)]

    def first_half(r):
        inner(2 * r)
        known(r)
        receive(r, 0)
        add_x(2 * r)
        outer(2 * r, whole, "plain")
        inner(2 * r + 1)

    def round_(r, carry):
        first_half(r)

        @pl.when(r == 0)
        def _():
            co_copy().wait_recv()
            ct_copy(0).wait_recv()
            ct_copy(1).wait_recv()
            for way in range(2):
                @pl.when(sides[1 - way][1])
                def _():
                    cx_copy(way).wait_recv()

        complete(r)
        receive(r, 1)
        add_x(2 * r + 1)
        gathered = outer(2 * r + 1, middle, "round", nothing(3))
        complete_ends(r)
        gathered = outer(2 * r + 1, ends, "round", gathered)
        join(2 * r + 2, gathered)
        send(r + 1)

        @pl.when(r == 0)
        def _():
            loads[3].wait()

            def weigh(i, carry):
                length = width[i].astype(jnp.float32)
                inverse = 1.0 / (length * length)
                for shift in range(1, SEP + 1):
                    weights[shift - 1, i] = jnp.exp(-(shift * shift) * inverse)
                return carry

            lax.fori_loop(0, cells, weigh, 0)

        return carry

    lax.fori_loop(0, ROUNDS - 1, round_, 0)
    last = ROUNDS - 1
    first_half(last)
    complete(last)
    receive(last, 1)
    add_x(2 * last + 1)
    outer(2 * last + 1, middle, "none")
    for way in range(2):
        @pl.when(sides[way][1])
        def _():
            p_copy(way, 0).start()

    complete_ends(last)
    outer(2 * last + 1, ends, "none")
    for way in range(2):
        @pl.when(sides[way][1])
        def _():
            p_copy(way, 1).start()
            p_copy(way, 2).start()

    store = pltpu.make_async_copy(state.at[0], green, store_sem.at[0])
    store.start()
    loads[4].wait()
    for way in range(2):
        @pl.when(sides[1 - way][1])
        def _():
            for piece in range(3):
                p_copy(way, piece).wait_recv()

    def integrate(i, carry):
        re, im = pressure[0, cells + i], pressure[1, cells + i]
        sum_re, sum_im = re, im
        for shift in range(1, SEP + 1):
            w = weights[shift - 1, i]
            sum_re = sum_re + w * (pressure[0, cells + i + shift] + pressure[0, cells + i - shift])
            sum_im = sum_im + w * (pressure[1, cells + i + shift] + pressure[1, cells + i - shift])
        result[i] = amp[i] * (re * sum_re + im * sum_im)
        return carry

    lax.fori_loop(0, cells, integrate, 0)
    store_2 = pltpu.make_async_copy(result, intensity, store_sem.at[1])
    store_2.start()

    def drain(r, carry):
        for s in (2 * r, 2 * r + 1):
            o_copy(s).wait_send()
            for way in range(2):
                @pl.when(sides[way][1])
                def _():
                    x_copy(s, way).wait_send()

        for way in range(2):
            t_copy(r, 0, way).wait_send()
            t_copy(r, 1, way).wait_send()
            a_copy(r, way).wait_send()

            @pl.when(sides[way][1])
            def _():
                b_copy(r, way).wait_send()
                d_copy(r, way, 0).wait_send()
                d_copy(r, way, 1).wait_send()

        return carry

    lax.fori_loop(0, ROUNDS, drain, 0)
    co_copy().wait_send()
    for way in range(2):
        ct_copy(way).wait_send()

        @pl.when(sides[way][1])
        def _():
            cx_copy(way).wait_send()
            for piece in range(3):
                p_copy(way, piece).wait_send()

    store.wait()
    store_2.wait()


def hand_over(green, intensity, green_out, intensity_out, held, held_2, load_sem, store_sem):
    parts = [(green.at[n], held.at[n], green_out.at[n]) for n in range(5)] + [(intensity, held_2, intensity_out)]
    loads = [pltpu.make_async_copy(src, mid, load_sem.at[n]) for n, (src, mid, _) in enumerate(parts)]
    stores = [pltpu.make_async_copy(mid, dst, store_sem.at[n]) for n, (_, mid, dst) in enumerate(parts)]
    for load in loads:
        load.start()
    for load, store in zip(loads, stores):
        load.wait()
        store.start()
    for store in stores:
        store.wait()


def per_device(n_ax, n_az, adjoint, mean_flow, forcing, tke, half_width, start):
    cells, sector, radial = tke.shape
    block = (cells, sector, radial)
    tile = (sector, radial)
    f32 = jnp.float32
    any_spec = pl.BlockSpec(memory_space=pl.ANY)

    def dma(*shape):
        return pltpu.SemaphoreType.DMA(shape)

    def vmem(*shape):
        return pltpu.VMEM(shape, f32)

    results = pl.pallas_call(
        functools.partial(kernel, n_ax, n_az),
        out_shape=(
            jax.ShapeDtypeStruct(adjoint.shape, f32),
            jax.ShapeDtypeStruct(tke.shape, f32),
        ),
        in_specs=[pl.BlockSpec(memory_space=pltpu.SMEM)] + [any_spec] * 5,
        out_specs=(any_spec, any_spec),
        scratch_shapes=[
            vmem(3, 5, 2, *block),
            vmem(5, 2, *block),
            vmem(4, *block),
            vmem(2, *block),
            vmem(*block),
            vmem(*block),
            pltpu.VMEM(block, jnp.int32),
            vmem(SEP, *block),
            vmem(3, *block),
            vmem(*block),
            vmem(5, 2, cells + 2, *tile),
            vmem(SECTIONS, 6, *block),
            vmem(ROUNDS, 4, *block),
            vmem(SECTIONS, 2, 5, 2, *tile),
            vmem(SECTIONS, 2, 5, 2, *tile),
            vmem(SECTIONS, 4, *block),
            vmem(SECTIONS, *tile),
            vmem(SECTIONS, *tile),
            vmem(ROUNDS, 2, 10, *tile),
            vmem(ROUNDS, 2, 10, *tile),
            vmem(ROUNDS, *tile),
            vmem(*tile),
            vmem(ROUNDS, 2, *tile),
            vmem(ROUNDS, 2, *tile),
            vmem(2, 4, *tile),
            vmem(3, *block),
            vmem(2, *tile),
            vmem(2, *tile),
            vmem(2, 3 * cells, *tile),
            dma(5), dma(2),
            dma(SECTIONS, 2), dma(SECTIONS, 2),
            dma(SECTIONS, 2), dma(SECTIONS, 2),
            dma(SECTIONS), dma(SECTIONS),
            dma(2, 3), dma(2, 3),
            dma(ROUNDS, 2, 2), dma(ROUNDS, 2, 2),
            dma(ROUNDS, 2), dma(ROUNDS, 2),
            dma(ROUNDS, 2), dma(ROUNDS, 2),
            dma(2), dma(2),
            dma(2), dma(2),
            dma(1), dma(1),
        ],
        compiler_params=pltpu.CompilerParams(
            collective_id=0, has_side_effects=True, vmem_limit_bytes=60 * 2**20
        ),
    )(start, adjoint, mean_flow, forcing, tke, half_width)
    return pl.pallas_call(
        hand_over,
        out_shape=(
            jax.ShapeDtypeStruct(adjoint.shape, f32),
            jax.ShapeDtypeStruct(tke.shape, f32),
        ),
        in_specs=[any_spec] * 2,
        out_specs=(any_spec, any_spec),
        scratch_shapes=[vmem(5, 2, *block), vmem(*block), dma(6), dma(6)],
        compiler_params=pltpu.CompilerParams(vmem_limit_bytes=60 * 2**20),
    )(*results)


def solution(mesh):
    return jax.shard_map(
        functools.partial(per_device, mesh.shape["ax"], mesh.shape["az"]),
        mesh=mesh,
        in_specs=(
            P(None, None, "ax", "az", None),
            P(None, "ax", "az", None),
            P(None, "ax", "az", None),
            P("ax", "az", None),
            P("ax", "az", None),
            P(),
        ),
        out_specs=(P(None, None, "ax", "az", None), P("ax", "az", None)),
        check_vma=False,
    )
```

```python
import functools
import math

import jax
import jax.numpy as jnp
from jax import lax
from jax.experimental import pallas as pl
from jax.experimental.pallas import tpu as pltpu
from jax.sharding import PartitionSpec as P

SEP = 16
SECTIONS = 6
ROUNDS = 3
NAXIAL = 2048
FREQUENCY = 0.7
MESH = pl.DeviceIdType.MESH
CHUNK = 4


def lane_pack(lane, gathered, value, to):
    moved = value if to == 0 else pltpu.roll(value, to, 1)
    return jnp.where(lane == to, moved, gathered)


def kernel(
    n_ax, n_az,
    start, adjoint, mean_flow, forcing, tke, half_width,
    *refs,
):
    green, intensity = refs[:10], refs[10]
    (
        state, partial, coef, force, sigma, amp, width, weights, flow, result,
        flux_x, flux_l, part_l, send_x, recv_x, recv_t, send_o, recv_o,
        send_d, recv_d, recv_a, extra_o, send_p, recv_p, coef_x, coef_t, send_c, coef_o, pressure,
        load_sem, store_sem, x_send, x_recv, t_send, t_recv, o_send, o_recv, p_send, p_recv,
        d_send, d_recv, a_send, a_recv, b_send, b_recv, cx_send, cx_recv, ct_send, ct_recv, co_send, co_recv,
    ) = refs[11:]
    cells, sector, radial = state.shape[3], state.shape[4], state.shape[5]
    ax, az = lax.axis_index("ax"), lax.axis_index("az")
    half_turn = n_az // 2
    left, right = ax - 1, ax + 1
    below, above = lax.rem(az + n_az - 1, n_az), lax.rem(az + 1, n_az)
    opposite = lax.rem(az + half_turn, n_az)
    opposite_below, opposite_above = lax.rem(az + half_turn - 1, n_az), lax.rem(az + half_turn + 1, n_az)
    has_left, has_right = ax > 0, ax < n_ax - 1
    sides = ((right, has_right), (left, has_left))
    turns = ((above, sector - 1, 0), (below, 0, sector - 1))

    loads = [
        pltpu.make_async_copy(src, dst, load_sem.at[n])
        for n, (src, dst) in enumerate(
            [(mean_flow, flow), (adjoint, state.at[0]), (forcing, force), (half_width, width), (tke, amp)]
        )
    ]
    for load in loads:
        load.start()

    barrier = pltpu.get_barrier_semaphore()

    def greet(i, k):
        pl.semaphore_signal(barrier, inc=1, device_id=(i, k), device_id_type=MESH)

    for i, there in sides:
        @pl.when(there)
        def _():
            for k in (opposite, below, above, az):
                greet(i, k)

    for k in (opposite_below, opposite_above, opposite, below, above):
        greet(ax, k)

    step_t = 2 * math.pi / (sector * n_az)
    lane = lax.broadcasted_iota(jnp.int32, (sector, radial), 1)
    row = lax.broadcasted_iota(jnp.int32, (sector, radial), 0)
    radius = lane.astype(jnp.float32) + 0.5
    tau = 0.8 / (2.0 + 1.0 / (radius * step_t))
    turn = 0.5 / (step_t * radius)
    outward = jnp.where(lane == radial - 1, 0.0, 0.5 * (radius + 1.0) / radius)
    inward = jnp.where(lane == 0, 0.0, 0.5 * (radius - 1.0) / radius)
    up = jnp.where(row == sector - 1, 0.0, turn)
    down = jnp.where(row == 0, 0.0, turn)
    is_edge = (row == 0) | (row == sector - 1)
    is_axis = lane == 0
    edge = jnp.where(row == 0, -turn, jnp.where(row == sector - 1, turn, 0.0))
    tau_0 = 0.8 / (2.0 + 1.0 / (0.5 * step_t))
    turn_0 = 0.5 / (step_t * 0.5)
    edge_0 = jnp.where(row == 0, -turn_0, jnp.where(row == sector - 1, turn_0, 0.0))

    first = start[0] + ax * cells
    pos = first + lax.broadcasted_iota(jnp.int32, (cells, sector, radial), 0)
    sigma[...] = 0.5 * (pos.astype(jnp.float32) + 0.5) / NAXIAL

    flux_x[:, :, 0] = jnp.zeros((5, 2, sector, radial), jnp.float32)
    flux_x[:, :, cells + 1] = jnp.zeros((5, 2, sector, radial), jnp.float32)

    @pl.when(jnp.logical_not(has_left))
    def _():
        pressure[:, 0:cells] = jnp.zeros((2, cells, sector, radial), jnp.float32)

    @pl.when(jnp.logical_not(has_right))
    def _():
        pressure[:, 2 * cells : 3 * cells] = jnp.zeros((2, cells, sector, radial), jnp.float32)

    def remote(src, dst, send_sem, recv_sem, i, k):
        return pltpu.make_async_remote_copy(
            src_ref=src, dst_ref=dst, send_sem=send_sem, recv_sem=recv_sem,
            device_id=(i, k), device_id_type=MESH,
        )

    def t_copy(r, later, way):
        who, mine, its = turns[way]
        source = part_l.at[r] if later else flux_l.at[2 * r, pl.ds(0, 4)]
        s = 2 * r + later
        return remote(
            source.at[:, :, mine], recv_t.at[s, :, :, its], t_send.at[s, way], t_recv.at[s, way], ax, who
        )

    def x_copy(s, way):
        return remote(send_x.at[s, way], recv_x.at[s, way], x_send.at[s, way], x_recv.at[s, way], sides[way][0], az)

    def o_copy(s):
        return remote(send_o.at[s], recv_o.at[s], o_send.at[s], o_recv.at[s], ax, opposite)

    def d_copy(r, way, spin):
        who, mine, its = turns[spin]
        return remote(
            send_d.at[r, way, :, mine], recv_d.at[r, way, :, its],
            d_send.at[r, way, spin], d_recv.at[r, way, spin], sides[way][0], who,
        )

    def a_copy(r, spin):
        _, mine, its = turns[spin]
        return remote(
            send_o.at[2 * r, pl.ds(mine, 1)], recv_a.at[r, pl.ds(its, 1)], a_send.at[r, spin], a_recv.at[r, spin],
            ax, (opposite_above, opposite_below)[spin],
        )

    def b_copy(r, way):
        return remote(
            send_p.at[r, way], recv_p.at[r, way], b_send.at[r, way], b_recv.at[r, way], sides[way][0], opposite
        )

    def cx_copy(way):
        return remote(
            coef.at[:, (cells - 1, 0)[way]], coef_x.at[way], cx_send.at[way], cx_recv.at[way], sides[way][0], az
        )

    def ct_copy(way):
        who, mine, its = turns[way]
        return remote(
            coef.at[pl.ds(1, 3), :, mine], coef_t.at[:, :, its], ct_send.at[way], ct_recv.at[way], ax, who
        )

    def co_copy():
        return remote(send_c, coef_o, co_send.at[0], co_recv.at[0], ax, opposite)

    def p_copy(way, piece):
        first, count = ((1, cells - 2), (0, 1), (cells - 1, 1))[piece]
        return remote(
            pressure.at[:, pl.ds(cells + first, count)],
            pressure.at[:, pl.ds((0, 2 * cells)[way] + first, count)],
            p_send.at[way, piece], p_recv.at[way, piece], sides[way][0], az,
        )

    def axial(q, u, rho, stiff, inv):
        a, b, c, d, e = q
        return (u * a, rho * a + stiff * e + u * b, u * c, u * d, b * inv + u * e)

    def fluxes(s, i, q, gathered):
        count = q[0].shape[1]
        at = pl.ds(i, count)
        u, rho, stiff, inv = coef[0, at], coef[1, at], coef[2, at], coef[3, at]
        a, b, c, d, e = q
        shared = rho * a + stiff * e
        turned, spread = d * inv, c * inv
        along = (u * a, shared + u * b, u * c, u * d, b * inv + u * e)
        for n, f in enumerate(along):
            flux_x[n, :, pl.ds(i + 1, count)] = f
        flux_l[s, 0:2, at] = shared
        flux_l[s, 2:4, at] = turned
        flux_l[s, 4:6, at] = spread
        if gathered is None:
            return None
        r = s // 2
        for way, k in ((1, -i), (0, cells - 1 - i)):
            if 0 <= k < count:
                for n, f in enumerate(along):
                    send_x[s, way, n] = f[:, k]
                for n, f in enumerate((along[0], along[3], along[4], shared, turned)):
                    send_d[r, way, 2 * n : 2 * n + 2] = f[:, k]
                packed = jnp.zeros((sector, radial), jnp.float32)
                for n, f in enumerate((shared, spread, along[0], along[2], along[4])):
                    for part in range(2):
                        packed = lane_pack(lane, packed, f[part, k], 2 * n + part)
                send_p[r, way] = packed
        for n, f in enumerate((shared, spread, turned)):
            for part in range(2):
                for k in range(count):
                    gathered[n] = lane_pack(lane, gathered[n], f[part, k], (2 * n + part) * cells + i + k)
        return gathered

    def nothing(count):
        return [jnp.zeros((sector, radial), jnp.float32) for _ in range(count)]

    def known(r):
        s = 2 * r + 1
        gathered = nothing(2)
        for i in range(0, cells, CHUNK):
            at = pl.ds(i, CHUNK)
            rho, stiff, inv = coef[1, at], coef[2, at], coef[3, at]
            shared = rho * partial[0, :, at] + stiff * partial[4, :, at]
            spread = partial[2, :, at] * inv
            part_l[r, 0:2, at] = shared
            part_l[r, 2:4, at] = partial[3, :, at] * inv
            for n, f in enumerate((shared, spread)):
                for part in range(2):
                    for k in range(CHUNK):
                        gathered[n] = lane_pack(lane, gathered[n], f[part, k], (2 * n + part) * cells + i + k)
        send_o[s] = jnp.where(lane < 2 * cells, gathered[0], gathered[1])
        o_copy(s).start()
        t_copy(r, 1, 0).start()
        t_copy(r, 1, 1).start()
        for way, i in ((1, 0), (0, cells - 1)):
            q = [partial[n, :, i] for n in range(5)]
            for n, f in enumerate(axial(q, coef[0, i], coef[1, i], coef[2, i], coef[3, i])):
                send_x[s, way, n] = f
        for way in range(2):
            @pl.when(sides[way][1])
            def _():
                x_copy(s, way).start()

    def send(r):
        for way in range(2):
            @pl.when(sides[way][1])
            def _():
                b_copy(r, way).start()

        a_copy(r, 0).start()
        a_copy(r, 1).start()
        o_copy(2 * r).start()
        for way in range(2):
            @pl.when(sides[way][1])
            def _():
                d_copy(r, way, 0).start()
                d_copy(r, way, 1).start()

        t_copy(r, 0, 0).start()
        t_copy(r, 0, 1).start()
        for way in range(2):
            @pl.when(sides[way][1])
            def _():
                x_copy(2 * r, way).start()

    def weight_of(s):
        third = lax.rem(s, 3)
        return jnp.where(third == 0, 1.0 / 3.0, jnp.where(third == 1, 0.5, 1.0))

    def inner(s):
        source = lax.rem(s, 3)
        scale = weight_of(s) * tau

        half = 0.5 * scale
        turned_by = scale * FREQUENCY

        def radially(f):
            return outward * pltpu.roll(f, radial - 1, 3) - inward * pltpu.roll(f, 1, 3)

        def around(f):
            return up * pltpu.roll(f, sector - 1, 2) - down * pltpu.roll(f, 1, 2)

        for i in range(0, cells, CHUNK):
            at = pl.ds(i, CHUNK)
            fade = scale * sigma[at]
            shared, turned, spread = flux_l[s, 0:2, at], flux_l[s, 2:4, at], flux_l[s, 4:6, at]
            extra = (None, None, radially(shared), around(shared), radially(spread) + around(turned) + force[:, at])
            for n in range(5):
                q = state[source, n, :, at]
                total = state[0, n, :, at] + half * (flux_x[n, :, pl.ds(i + 2, CHUNK)] - flux_x[n, :, at]) - fade * q
                if extra[n] is not None:
                    total = total + scale * extra[n]
                partial[n, 0, at] = total[0] + turned_by * q[1]
                partial[n, 1, at] = total[1] - turned_by * q[0]

    def receive(r, later):
        s = 2 * r + later
        for way in range(2):
            @pl.when(sides[1 - way][1])
            def _():
                x_copy(s, way).wait_recv()

        t_copy(r, later, 0).wait_recv()
        t_copy(r, later, 1).wait_recv()
        o_copy(s).wait_recv()

    def complete(r):
        scale, scale_0 = weight_of(2 * r) * tau, weight_of(2 * r) * tau_0
        half, half_0 = 0.5 * scale, 0.5 * scale_0
        around = scale * edge
        scale_2 = weight_of(2 * r + 1) * tau
        rows = scale_2 * edge
        a_copy(r, 0).wait_recv()
        a_copy(r, 1).wait_recv()
        aside = jnp.where(is_edge, recv_a[r], 0.0)
        axis = -half_0 * aside

        for i in range(0, cells, CHUNK):
            at = pl.ds(i, CHUNK)
            spun = jnp.stack(
                [
                    jnp.stack(
                        [
                            jnp.where(is_axis, pltpu.roll(axis, radial - (2 + part) * cells - i - k, 1), 0.0)
                            for k in range(CHUNK)
                        ]
                    )
                    for part in range(2)
                ]
            )
            more_d = -around * flux_l[2 * r, 0:2, at]
            more_e = spun - around * flux_l[2 * r, 2:4, at]
            partial[3, :, at] = partial[3, :, at] + rows * jnp.where(is_edge, coef_t[1, at] * more_e, 0.0)
            partial[4, :, at] = partial[4, :, at] + rows * jnp.where(is_edge, coef_t[2, at] * more_d, 0.0)

        mine = send_o[2 * r]
        more_c = -half_0 * pltpu.roll(mine, 2 * cells, 1)
        more_e = -half_0 * pltpu.roll(mine, radial - 2 * cells, 1) + scale_0 * edge_0 * pltpu.roll(
            aside, radial - 4 * cells, 1
        )
        extra_o[...] = coef_o[0] * jnp.where(lane < 2 * cells, 0.0, more_c) + coef_o[1] * jnp.where(
            lane < 2 * cells, more_e, 0.0
        )

        for way, i, sign in ((0, 0, 1.0), (1, cells - 1, -1.0)):
            @pl.when(sides[1 - way][1])
            def _():
                d_copy(r, way, 0).wait_recv()
                d_copy(r, way, 1).wait_recv()
                corner = jnp.where(is_edge, recv_d[r, way], 0.0)
                gone = (-sign * half) * corner[0:6]
                more = [(sign * half) * send_x[2 * r, 1 - way, n] for n in range(5)]
                more[3] = more[3] + around * corner[6:8]
                more[4] = more[4] + around * corner[8:10]
                c = coef_x[way]
                along = axial(more, c[0], c[1], c[2], c[3])
                turned = [None, None, None]
                turned += [rows * jnp.where(is_edge, coef_t[0, i] * gone[0:2] + coef_t[1, i] * gone[4:6], 0.0)]
                turned += [rows * jnp.where(is_edge, coef_t[2, i] * gone[2:4], 0.0)]
                for n in range(5):
                    q = partial[n, :, i] - (0.5 * sign * scale_2) * along[n]
                    partial[n, :, i] = q if turned[n] is None else q + turned[n]

    def complete_ends(r):
        half_0 = (0.5 * tau_0) * weight_of(2 * r)
        half = (0.5 * weight_of(2 * r + 1)) * tau
        for way, i, sign in ((0, 0, 1.0), (1, cells - 1, -1.0)):
            @pl.when(sides[1 - way][1])
            def _():
                b_copy(r, way).wait_recv()
                packed = -half_0 * recv_p[r, way]

                def at_axis(n):
                    return jnp.stack(
                        [
                            jnp.where(is_axis, packed if n + part == 0 else pltpu.roll(packed, radial - n - part, 1), 0.0)
                            for part in range(2)
                        ]
                    )

                c, e = (-sign * half) * at_axis(0), (-sign * half) * at_axis(2)
                u, stiff = coef_x[way, 0], coef_x[way, 2]
                partial[1, :, i] = partial[1, :, i] + stiff * e
                partial[2, :, i] = partial[2, :, i] + u * c
                partial[4, :, i] = partial[4, :, i] + u * e

                def spread_out(n, to):
                    low = pltpu.roll(packed, (radial + to + i - n) % radial, 1)
                    high = pltpu.roll(packed, (radial + to + cells + i - n - 1) % radial, 1)
                    return jnp.where(lane == to + i, low, jnp.where(lane == to + cells + i, high, 0.0))

                extra_o[...] = extra_o[...] + sign * (
                    coef_o[0] * (spread_out(4, 0) + spread_out(6, 2 * cells)) + coef_o[1] * spread_out(8, 0)
                )

    def add_x(s):
        half = (0.5 * weight_of(s)) * tau
        for way, i, sign in ((0, 0, -1.0), (1, cells - 1, 1.0)):
            @pl.when(sides[1 - way][1])
            def _():
                partial[:, :, i] = partial[:, :, i] + (sign * half) * recv_x[s, way]

    def outer(s, chunks, then, gathered=None):
        scale = weight_of(s) * tau
        rows = scale * edge
        mirror = recv_o[s] if then == "plain" else recv_o[s] + extra_o[...]
        mirror = (-0.5 * tau_0) * weight_of(s) * mirror
        target = lax.rem(s + 1, 3)
        for i, count in chunks:
            at = pl.ds(i, count)
            q = [partial[n, :, at] for n in range(5)]
            ring = jnp.where(is_edge, recv_t[s, :, at], 0.0) * rows
            spun = [
                jnp.stack(
                    [
                        jnp.stack(
                            [
                                jnp.where(is_axis, pltpu.roll(mirror, (radial - n * cells - i - k) % radial, 1), 0.0)
                                for k in range(count)
                            ]
                        )
                        for n in (c, c + 1)
                    ]
                )
                for c in (0, 2)
            ]
            q[2] = q[2] + spun[0]
            q[3] = q[3] + ring[0:2]
            q[4] = q[4] + ring[2:4] + spun[1]
            for n in range(5):
                state[target, n, :, at] = q[n]
            if then == "none":
                pressure[:, pl.ds(cells + i, count)] = q[4]
            else:
                gathered = fluxes(s + 1, i, q, gathered)
        return gathered

    def join(s, gathered):
        send_o[s] = jnp.where(lane < 2 * cells, gathered[0], jnp.where(lane < 4 * cells, gathered[1], gathered[2]))

    loads[0].wait()
    rho = flow[1]
    coef[0] = flow[0]
    coef[1] = rho
    coef[2] = rho * flow[2]
    coef[3] = 1.0 / rho
    loads[1].wait()
    gathered = nothing(3)
    for i in range(0, cells, CHUNK):
        gathered = fluxes(0, i, [state[0, n, :, pl.ds(i, CHUNK)] for n in range(5)], gathered)
    join(0, gathered)

    there = has_left.astype(jnp.int32) + has_right.astype(jnp.int32)
    pl.semaphore_wait(barrier, 5 + 4 * there)
    send(0)

    gathered = nothing(3)
    for n, which in enumerate((1, 3, 2)):
        for i in range(cells):
            gathered[n] = lane_pack(lane, gathered[n], coef[which, i], (0, 2, 0)[n] * cells + i)
    wide = [jnp.where(lane % (2 * cells) < cells, g, pltpu.roll(g, cells, 1)) for g in gathered]
    send_c[0] = jnp.where(lane < 2 * cells, wide[0], jnp.where(lane < 4 * cells, wide[1], 0.0))
    send_c[1] = jnp.where(lane < 2 * cells, wide[2], 0.0)
    co_copy().start()
    ct_copy(0).start()
    ct_copy(1).start()
    for way in range(2):
        @pl.when(sides[way][1])
        def _():
            cx_copy(way).start()

    loads[2].wait()
    whole = [(i, CHUNK) for i in range(0, cells, CHUNK)]
    middle = [(i, min(CHUNK, cells - 1 - i)) for i in range(1, cells - 1, CHUNK)]
    ends = [(0, 1), (cells - 1, 1)]

    def first_half(r):
        inner(2 * r)
        known(r)
        receive(r, 0)
        add_x(2 * r)
        outer(2 * r, whole, "plain")
        inner(2 * r + 1)

    def round_(r, carry):
        first_half(r)

        @pl.when(r == 0)
        def _():
            co_copy().wait_recv()
            ct_copy(0).wait_recv()
            ct_copy(1).wait_recv()
            for way in range(2):
                @pl.when(sides[1 - way][1])
                def _():
                    cx_copy(way).wait_recv()

        complete(r)
        receive(r, 1)
        add_x(2 * r + 1)
        gathered = outer(2 * r + 1, middle, "round", nothing(3))
        complete_ends(r)
        gathered = outer(2 * r + 1, ends, "round", gathered)
        join(2 * r + 2, gathered)
        send(r + 1)

        @pl.when(r == 0)
        def _():
            loads[3].wait()

            def weigh(i, carry):
                length = width[i].astype(jnp.float32)
                inverse = 1.0 / (length * length)
                for shift in range(1, SEP + 1):
                    weights[shift - 1, i] = jnp.exp(-(shift * shift) * inverse)
                return carry

            lax.fori_loop(0, cells, weigh, 0)

        return carry

    lax.fori_loop(0, ROUNDS - 1, round_, 0)
    last = ROUNDS - 1
    first_half(last)
    complete(last)
    receive(last, 1)
    add_x(2 * last + 1)
    outer(2 * last + 1, middle, "none")
    for way in range(2):
        @pl.when(sides[way][1])
        def _():
            p_copy(way, 0).start()

    complete_ends(last)
    outer(2 * last + 1, ends, "none")
    for way in range(2):
        @pl.when(sides[way][1])
        def _():
            p_copy(way, 1).start()
            p_copy(way, 2).start()

    stores = [pltpu.make_async_copy(state.at[0, n // 2, n % 2], green[n], store_sem.at[n]) for n in range(10)]
    for store in stores:
        store.start()
    loads[4].wait()
    for way in range(2):
        @pl.when(sides[1 - way][1])
        def _():
            for piece in range(3):
                p_copy(way, piece).wait_recv()

    def integrate(i, carry):
        re, im = pressure[0, cells + i], pressure[1, cells + i]
        sum_re, sum_im = re, im
        for shift in range(1, SEP + 1):
            w = weights[shift - 1, i]
            sum_re = sum_re + w * (pressure[0, cells + i + shift] + pressure[0, cells + i - shift])
            sum_im = sum_im + w * (pressure[1, cells + i + shift] + pressure[1, cells + i - shift])
        result[i] = amp[i] * (re * sum_re + im * sum_im)
        return carry

    lax.fori_loop(0, cells, integrate, 0)
    stores.append(pltpu.make_async_copy(result, intensity, store_sem.at[10]))
    stores[10].start()

    def drain(r, carry):
        for s in (2 * r, 2 * r + 1):
            o_copy(s).wait_send()
            for way in range(2):
                @pl.when(sides[way][1])
                def _():
                    x_copy(s, way).wait_send()

        for way in range(2):
            t_copy(r, 0, way).wait_send()
            t_copy(r, 1, way).wait_send()
            a_copy(r, way).wait_send()

            @pl.when(sides[way][1])
            def _():
                b_copy(r, way).wait_send()
                d_copy(r, way, 0).wait_send()
                d_copy(r, way, 1).wait_send()

        return carry

    lax.fori_loop(0, ROUNDS, drain, 0)
    co_copy().wait_send()
    for way in range(2):
        ct_copy(way).wait_send()

        @pl.when(sides[way][1])
        def _():
            cx_copy(way).wait_send()
            for piece in range(3):
                p_copy(way, piece).wait_send()

    for store in stores:
        store.wait()


def hand_over(*refs):
    fields, (green, intensity, sem) = refs[:11], refs[11:]
    places = [green.at[n // 2, n % 2] for n in range(10)] + [intensity]
    copies = [pltpu.make_async_copy(src, dst, sem.at[n]) for n, (src, dst) in enumerate(zip(fields, places))]
    for copy in copies:
        copy.start()
    for copy in copies:
        copy.wait()


def per_device(n_ax, n_az, adjoint, mean_flow, forcing, tke, half_width, start):
    cells, sector, radial = tke.shape
    block = (cells, sector, radial)
    tile = (sector, radial)
    f32 = jnp.float32
    any_spec = pl.BlockSpec(memory_space=pl.ANY)

    def dma(*shape):
        return pltpu.SemaphoreType.DMA(shape)

    def vmem(*shape):
        return pltpu.VMEM(shape, f32)

    results = pl.pallas_call(
        functools.partial(kernel, n_ax, n_az),
        out_shape=[jax.ShapeDtypeStruct(block, f32)] * 11,
        in_specs=[pl.BlockSpec(memory_space=pltpu.SMEM)] + [any_spec] * 5,
        out_specs=[any_spec] * 11,
        scratch_shapes=[
            vmem(3, 5, 2, *block),
            vmem(5, 2, *block),
            vmem(4, *block),
            vmem(2, *block),
            vmem(*block),
            vmem(*block),
            pltpu.VMEM(block, jnp.int32),
            vmem(SEP, *block),
            vmem(3, *block),
            vmem(*block),
            vmem(5, 2, cells + 2, *tile),
            vmem(SECTIONS, 6, *block),
            vmem(ROUNDS, 4, *block),
            vmem(SECTIONS, 2, 5, 2, *tile),
            vmem(SECTIONS, 2, 5, 2, *tile),
            vmem(SECTIONS, 4, *block),
            vmem(SECTIONS, *tile),
            vmem(SECTIONS, *tile),
            vmem(ROUNDS, 2, 10, *tile),
            vmem(ROUNDS, 2, 10, *tile),
            vmem(ROUNDS, *tile),
            vmem(*tile),
            vmem(ROUNDS, 2, *tile),
            vmem(ROUNDS, 2, *tile),
            vmem(2, 4, *tile),
            vmem(3, *block),
            vmem(2, *tile),
            vmem(2, *tile),
            vmem(2, 3 * cells, *tile),
            dma(5), dma(11),
            dma(SECTIONS, 2), dma(SECTIONS, 2),
            dma(SECTIONS, 2), dma(SECTIONS, 2),
            dma(SECTIONS), dma(SECTIONS),
            dma(2, 3), dma(2, 3),
            dma(ROUNDS, 2, 2), dma(ROUNDS, 2, 2),
            dma(ROUNDS, 2), dma(ROUNDS, 2),
            dma(ROUNDS, 2), dma(ROUNDS, 2),
            dma(2), dma(2),
            dma(2), dma(2),
            dma(1), dma(1),
        ],
        compiler_params=pltpu.CompilerParams(
            collective_id=0, has_side_effects=True, vmem_limit_bytes=54528 * 1024
        ),
    )(start, adjoint, mean_flow, forcing, tke, half_width)
    return pl.pallas_call(
        hand_over,
        out_shape=(
            jax.ShapeDtypeStruct(adjoint.shape, f32),
            jax.ShapeDtypeStruct(tke.shape, f32),
        ),
        in_specs=[any_spec] * 11,
        out_specs=(any_spec, any_spec),
        scratch_shapes=[dma(11)],
        compiler_params=pltpu.CompilerParams(vmem_limit_bytes=2**20),
    )(*results)


def solution(mesh):
    return jax.shard_map(
        functools.partial(per_device, mesh.shape["ax"], mesh.shape["az"]),
        mesh=mesh,
        in_specs=(
            P(None, None, "ax", "az", None),
            P(None, "ax", "az", None),
            P(None, "ax", "az", None),
            P("ax", "az", None),
            P("ax", "az", None),
            P(),
        ),
        out_specs=(P(None, None, "ax", "az", None), P("ax", "az", None)),
        check_vma=False,
    )
```

```python
import functools
import math

import jax
import jax.numpy as jnp
from jax import lax
from jax.experimental import pallas as pl
from jax.experimental.pallas import tpu as pltpu
from jax.sharding import PartitionSpec as P

SEP = 16
SECTIONS = 6
ROUNDS = 3
NAXIAL = 2048
FREQUENCY = 0.7
MESH = pl.DeviceIdType.MESH
CHUNK = 4


def lane_pack(lane, gathered, value, to):
    moved = value if to == 0 else pltpu.roll(value, to, 1)
    return jnp.where(lane == to, moved, gathered)


def kernel(
    n_ax, n_az,
    start, adjoint, mean_flow, forcing, tke, half_width,
    *refs,
):
    green, intensity = refs[:10], refs[10]
    (
        state, partial, coef, force, sigma, amp, width, weights, flow, result,
        flux_x, flux_l, part_l, send_x, recv_x, recv_t, send_o, recv_o,
        send_d, recv_d, recv_a, extra_o, send_p, recv_p, coef_x, coef_t, send_c, coef_o, pressure,
        load_sem, store_sem, x_send, x_recv, t_send, t_recv, o_send, o_recv, p_send, p_recv,
        d_send, d_recv, a_send, a_recv, b_send, b_recv, cx_send, cx_recv, ct_send, ct_recv, co_send, co_recv,
    ) = refs[11:]
    cells, sector, radial = state.shape[3], state.shape[4], state.shape[5]
    ax, az = lax.axis_index("ax"), lax.axis_index("az")
    half_turn = n_az // 2
    left, right = ax - 1, ax + 1
    below, above = lax.rem(az + n_az - 1, n_az), lax.rem(az + 1, n_az)
    opposite = lax.rem(az + half_turn, n_az)
    opposite_below, opposite_above = lax.rem(az + half_turn - 1, n_az), lax.rem(az + half_turn + 1, n_az)
    has_left, has_right = ax > 0, ax < n_ax - 1
    sides = ((right, has_right), (left, has_left))
    turns = ((above, sector - 1, 0), (below, 0, sector - 1))

    loads = [
        pltpu.make_async_copy(src, dst, load_sem.at[n])
        for n, (src, dst) in enumerate(
            [(mean_flow, flow), (adjoint, state.at[0]), (forcing, force), (half_width, width), (tke, amp)]
        )
    ]
    for load in loads:
        load.start()

    barrier = pltpu.get_barrier_semaphore()

    def greet(i, k):
        pl.semaphore_signal(barrier, inc=1, device_id=(i, k), device_id_type=MESH)

    for i, there in sides:
        @pl.when(there)
        def _():
            for k in (opposite, below, above, az):
                greet(i, k)

    for k in (opposite_below, opposite_above, opposite, below, above):
        greet(ax, k)

    step_t = 2 * math.pi / (sector * n_az)
    lane = lax.broadcasted_iota(jnp.int32, (sector, radial), 1)
    row = lax.broadcasted_iota(jnp.int32, (sector, radial), 0)
    radius = lane.astype(jnp.float32) + 0.5
    tau = 0.8 / (2.0 + 1.0 / (radius * step_t))
    turn = 0.5 / (step_t * radius)
    outward = jnp.where(lane == radial - 1, 0.0, 0.5 * (radius + 1.0) / radius)
    inward = jnp.where(lane == 0, 0.0, 0.5 * (radius - 1.0) / radius)
    up = jnp.where(row == sector - 1, 0.0, turn)
    down = jnp.where(row == 0, 0.0, turn)
    is_edge = (row == 0) | (row == sector - 1)
    is_axis = lane == 0
    edge = jnp.where(row == 0, -turn, jnp.where(row == sector - 1, turn, 0.0))
    tau_0 = 0.8 / (2.0 + 1.0 / (0.5 * step_t))
    turn_0 = 0.5 / (step_t * 0.5)
    edge_0 = jnp.where(row == 0, -turn_0, jnp.where(row == sector - 1, turn_0, 0.0))

    first = start[0] + ax * cells
    pos = first + lax.broadcasted_iota(jnp.int32, (cells, sector, radial), 0)
    sigma[...] = 0.5 * (pos.astype(jnp.float32) + 0.5) / NAXIAL

    flux_x[:, :, 0] = jnp.zeros((5, 2, sector, radial), jnp.float32)
    flux_x[:, :, cells + 1] = jnp.zeros((5, 2, sector, radial), jnp.float32)

    @pl.when(jnp.logical_not(has_left))
    def _():
        pressure[:, 0:cells] = jnp.zeros((2, cells, sector, radial), jnp.float32)

    @pl.when(jnp.logical_not(has_right))
    def _():
        pressure[:, 2 * cells : 3 * cells] = jnp.zeros((2, cells, sector, radial), jnp.float32)

    def remote(src, dst, send_sem, recv_sem, i, k):
        return pltpu.make_async_remote_copy(
            src_ref=src, dst_ref=dst, send_sem=send_sem, recv_sem=recv_sem,
            device_id=(i, k), device_id_type=MESH,
        )

    def t_copy(r, later, way):
        who, mine, its = turns[way]
        source = part_l.at[r] if later else flux_l.at[2 * r, pl.ds(0, 4)]
        s = 2 * r + later
        return remote(
            source.at[:, :, mine], recv_t.at[s, :, :, its], t_send.at[s, way], t_recv.at[s, way], ax, who
        )

    def x_copy(s, way):
        return remote(send_x.at[s, way], recv_x.at[s, way], x_send.at[s, way], x_recv.at[s, way], sides[way][0], az)

    def o_copy(s):
        return remote(send_o.at[s], recv_o.at[s], o_send.at[s], o_recv.at[s], ax, opposite)

    def d_copy(r, way, spin):
        who, mine, its = turns[spin]
        return remote(
            send_d.at[r, way, :, mine], recv_d.at[r, way, :, its],
            d_send.at[r, way, spin], d_recv.at[r, way, spin], sides[way][0], who,
        )

    def a_copy(r, spin):
        _, mine, its = turns[spin]
        return remote(
            send_o.at[2 * r, pl.ds(mine, 1)], recv_a.at[r, pl.ds(its, 1)], a_send.at[r, spin], a_recv.at[r, spin],
            ax, (opposite_above, opposite_below)[spin],
        )

    def b_copy(r, way):
        return remote(
            send_p.at[r, way], recv_p.at[r, way], b_send.at[r, way], b_recv.at[r, way], sides[way][0], opposite
        )

    def cx_copy(way):
        return remote(
            coef.at[:, (cells - 1, 0)[way]], coef_x.at[way], cx_send.at[way], cx_recv.at[way], sides[way][0], az
        )

    def ct_copy(way):
        who, mine, its = turns[way]
        return remote(
            coef.at[pl.ds(1, 3), :, mine], coef_t.at[:, :, its], ct_send.at[way], ct_recv.at[way], ax, who
        )

    def co_copy():
        return remote(send_c, coef_o, co_send.at[0], co_recv.at[0], ax, opposite)

    def p_copy(way, piece):
        first, count = ((1, cells - 2), (0, 1), (cells - 1, 1))[piece]
        return remote(
            pressure.at[:, pl.ds(cells + first, count)],
            pressure.at[:, pl.ds((0, 2 * cells)[way] + first, count)],
            p_send.at[way, piece], p_recv.at[way, piece], sides[way][0], az,
        )

    def axial(q, u, rho, stiff, inv):
        a, b, c, d, e = q
        return (u * a, rho * a + stiff * e + u * b, u * c, u * d, b * inv + u * e)

    def fluxes(s, i, q, gathered):
        count = q[0].shape[1]
        at = pl.ds(i, count)
        u, rho, stiff, inv = coef[0, at], coef[1, at], coef[2, at], coef[3, at]
        a, b, c, d, e = q
        shared = rho * a + stiff * e
        turned, spread = d * inv, c * inv
        along = (u * a, shared + u * b, u * c, u * d, b * inv + u * e)
        for n, f in enumerate(along):
            flux_x[n, :, pl.ds(i + 1, count)] = f
        flux_l[s, 0:2, at] = shared
        flux_l[s, 2:4, at] = turned
        flux_l[s, 4:6, at] = spread
        if gathered is None:
            return None
        r = s // 2
        for way, k in ((1, -i), (0, cells - 1 - i)):
            if 0 <= k < count:
                for n, f in enumerate(along):
                    send_x[s, way, n] = f[:, k]
                for n, f in enumerate((along[0], along[3], along[4], shared, turned)):
                    send_d[r, way, 2 * n : 2 * n + 2] = f[:, k]
                packed = jnp.zeros((sector, radial), jnp.float32)
                for n, f in enumerate((shared, spread, along[0], along[2], along[4])):
                    for part in range(2):
                        packed = lane_pack(lane, packed, f[part, k], 2 * n + part)
                send_p[r, way] = packed
        for n, f in enumerate((shared, spread, turned)):
            for part in range(2):
                for k in range(count):
                    gathered[n] = lane_pack(lane, gathered[n], f[part, k], (2 * n + part) * cells + i + k)
        return gathered

    def nothing(count):
        return [jnp.zeros((sector, radial), jnp.float32) for _ in range(count)]

    def known(r):
        s = 2 * r + 1
        gathered = nothing(2)
        for i in range(0, cells, CHUNK):
            at = pl.ds(i, CHUNK)
            rho, stiff, inv = coef[1, at], coef[2, at], coef[3, at]
            shared = rho * partial[0, :, at] + stiff * partial[4, :, at]
            spread = partial[2, :, at] * inv
            part_l[r, 0:2, at] = shared
            part_l[r, 2:4, at] = partial[3, :, at] * inv
            for n, f in enumerate((shared, spread)):
                for part in range(2):
                    for k in range(CHUNK):
                        gathered[n] = lane_pack(lane, gathered[n], f[part, k], (2 * n + part) * cells + i + k)
        send_o[s] = jnp.where(lane < 2 * cells, gathered[0], gathered[1])
        o_copy(s).start()
        t_copy(r, 1, 0).start()
        t_copy(r, 1, 1).start()
        for way, i in ((1, 0), (0, cells - 1)):
            q = [partial[n, :, i] for n in range(5)]
            for n, f in enumerate(axial(q, coef[0, i], coef[1, i], coef[2, i], coef[3, i])):
                send_x[s, way, n] = f
        for way in range(2):
            @pl.when(sides[way][1])
            def _():
                x_copy(s, way).start()

    def send(r):
        for way in range(2):
            @pl.when(sides[way][1])
            def _():
                b_copy(r, way).start()

        a_copy(r, 0).start()
        a_copy(r, 1).start()
        o_copy(2 * r).start()
        for way in range(2):
            @pl.when(sides[way][1])
            def _():
                d_copy(r, way, 0).start()
                d_copy(r, way, 1).start()

        t_copy(r, 0, 0).start()
        t_copy(r, 0, 1).start()
        for way in range(2):
            @pl.when(sides[way][1])
            def _():
                x_copy(2 * r, way).start()

    def weight_of(s):
        third = lax.rem(s, 3)
        return jnp.where(third == 0, 1.0 / 3.0, jnp.where(third == 1, 0.5, 1.0))

    def inner(s):
        source = lax.rem(s, 3)
        scale = weight_of(s) * tau

        half = 0.5 * scale
        turned_by = scale * FREQUENCY

        def radially(f):
            return outward * pltpu.roll(f, radial - 1, 3) - inward * pltpu.roll(f, 1, 3)

        def around(f):
            return up * pltpu.roll(f, sector - 1, 2) - down * pltpu.roll(f, 1, 2)

        for i in range(0, cells, CHUNK):
            at = pl.ds(i, CHUNK)
            fade = scale * sigma[at]
            shared, turned, spread = flux_l[s, 0:2, at], flux_l[s, 2:4, at], flux_l[s, 4:6, at]
            extra = (None, None, radially(shared), around(shared), radially(spread) + around(turned) + force[:, at])
            for n in range(5):
                q = state[source, n, :, at]
                total = state[0, n, :, at] + half * (flux_x[n, :, pl.ds(i + 2, CHUNK)] - flux_x[n, :, at]) - fade * q
                if extra[n] is not None:
                    total = total + scale * extra[n]
                partial[n, 0, at] = total[0] + turned_by * q[1]
                partial[n, 1, at] = total[1] - turned_by * q[0]

    def receive(r, later):
        s = 2 * r + later
        for way in range(2):
            @pl.when(sides[1 - way][1])
            def _():
                x_copy(s, way).wait_recv()

        t_copy(r, later, 0).wait_recv()
        t_copy(r, later, 1).wait_recv()
        o_copy(s).wait_recv()

    def complete(r):
        scale, scale_0 = weight_of(2 * r) * tau, weight_of(2 * r) * tau_0
        half, half_0 = 0.5 * scale, 0.5 * scale_0
        around = scale * edge
        scale_2 = weight_of(2 * r + 1) * tau
        rows = scale_2 * edge
        a_copy(r, 0).wait_recv()
        a_copy(r, 1).wait_recv()
        aside = jnp.where(is_edge, recv_a[r], 0.0)
        axis = -half_0 * aside

        for i in range(0, cells, CHUNK):
            at = pl.ds(i, CHUNK)
            spun = jnp.stack(
                [
                    jnp.stack(
                        [
                            jnp.where(is_axis, pltpu.roll(axis, radial - (2 + part) * cells - i - k, 1), 0.0)
                            for k in range(CHUNK)
                        ]
                    )
                    for part in range(2)
                ]
            )
            more_d = -around * flux_l[2 * r, 0:2, at]
            more_e = spun - around * flux_l[2 * r, 2:4, at]
            partial[3, :, at] = partial[3, :, at] + rows * jnp.where(is_edge, coef_t[1, at] * more_e, 0.0)
            partial[4, :, at] = partial[4, :, at] + rows * jnp.where(is_edge, coef_t[2, at] * more_d, 0.0)

        mine = send_o[2 * r]
        more_c = -half_0 * pltpu.roll(mine, 2 * cells, 1)
        more_e = -half_0 * pltpu.roll(mine, radial - 2 * cells, 1) + scale_0 * edge_0 * pltpu.roll(
            aside, radial - 4 * cells, 1
        )
        extra_o[...] = coef_o[0] * jnp.where(lane < 2 * cells, 0.0, more_c) + coef_o[1] * jnp.where(
            lane < 2 * cells, more_e, 0.0
        )

        for way, i, sign in ((0, 0, 1.0), (1, cells - 1, -1.0)):
            @pl.when(sides[1 - way][1])
            def _():
                d_copy(r, way, 0).wait_recv()
                d_copy(r, way, 1).wait_recv()
                corner = jnp.where(is_edge, recv_d[r, way], 0.0)
                gone = (-sign * half) * corner[0:6]
                more = [(sign * half) * send_x[2 * r, 1 - way, n] for n in range(5)]
                more[3] = more[3] + around * corner[6:8]
                more[4] = more[4] + around * corner[8:10]
                c = coef_x[way]
                along = axial(more, c[0], c[1], c[2], c[3])
                turned = [None, None, None]
                turned += [rows * jnp.where(is_edge, coef_t[0, i] * gone[0:2] + coef_t[1, i] * gone[4:6], 0.0)]
                turned += [rows * jnp.where(is_edge, coef_t[2, i] * gone[2:4], 0.0)]
                for n in range(5):
                    q = partial[n, :, i] - (0.5 * sign * scale_2) * along[n]
                    partial[n, :, i] = q if turned[n] is None else q + turned[n]

    def complete_ends(r):
        half_0 = (0.5 * tau_0) * weight_of(2 * r)
        half = (0.5 * weight_of(2 * r + 1)) * tau
        for way, i, sign in ((0, 0, 1.0), (1, cells - 1, -1.0)):
            @pl.when(sides[1 - way][1])
            def _():
                b_copy(r, way).wait_recv()
                packed = -half_0 * recv_p[r, way]

                def at_axis(n):
                    return jnp.stack(
                        [
                            jnp.where(is_axis, packed if n + part == 0 else pltpu.roll(packed, radial - n - part, 1), 0.0)
                            for part in range(2)
                        ]
                    )

                c, e = (-sign * half) * at_axis(0), (-sign * half) * at_axis(2)
                u, stiff = coef_x[way, 0], coef_x[way, 2]
                partial[1, :, i] = partial[1, :, i] + stiff * e
                partial[2, :, i] = partial[2, :, i] + u * c
                partial[4, :, i] = partial[4, :, i] + u * e

                def spread_out(n, to):
                    low = pltpu.roll(packed, (radial + to + i - n) % radial, 1)
                    high = pltpu.roll(packed, (radial + to + cells + i - n - 1) % radial, 1)
                    return jnp.where(lane == to + i, low, jnp.where(lane == to + cells + i, high, 0.0))

                extra_o[...] = extra_o[...] + sign * (
                    coef_o[0] * (spread_out(4, 0) + spread_out(6, 2 * cells)) + coef_o[1] * spread_out(8, 0)
                )

    def add_x(s):
        half = (0.5 * weight_of(s)) * tau
        for way, i, sign in ((0, 0, -1.0), (1, cells - 1, 1.0)):
            @pl.when(sides[1 - way][1])
            def _():
                partial[:, :, i] = partial[:, :, i] + (sign * half) * recv_x[s, way]

    def outer(s, chunks, then, gathered=None):
        scale = weight_of(s) * tau
        rows = scale * edge
        mirror = recv_o[s] if then == "plain" else recv_o[s] + extra_o[...]
        mirror = (-0.5 * tau_0) * weight_of(s) * mirror
        target = lax.rem(s + 1, 3)
        for i, count in chunks:
            at = pl.ds(i, count)
            q = [partial[n, :, at] for n in range(5)]
            ring = jnp.where(is_edge, recv_t[s, :, at], 0.0) * rows
            spun = [
                jnp.stack(
                    [
                        jnp.stack(
                            [
                                jnp.where(is_axis, pltpu.roll(mirror, (radial - n * cells - i - k) % radial, 1), 0.0)
                                for k in range(count)
                            ]
                        )
                        for n in (c, c + 1)
                    ]
                )
                for c in (0, 2)
            ]
            q[2] = q[2] + spun[0]
            q[3] = q[3] + ring[0:2]
            q[4] = q[4] + ring[2:4] + spun[1]
            for n in range(5):
                state[target, n, :, at] = q[n]
            if then == "none":
                pressure[:, pl.ds(cells + i, count)] = q[4]
            else:
                gathered = fluxes(s + 1, i, q, gathered)
        return gathered

    def join(s, gathered):
        send_o[s] = jnp.where(lane < 2 * cells, gathered[0], jnp.where(lane < 4 * cells, gathered[1], gathered[2]))

    loads[0].wait()
    rho = flow[1]
    coef[0] = flow[0]
    coef[1] = rho
    coef[2] = rho * flow[2]
    coef[3] = 1.0 / rho
    loads[1].wait()
    gathered = nothing(3)
    for i in range(0, cells, CHUNK):
        gathered = fluxes(0, i, [state[0, n, :, pl.ds(i, CHUNK)] for n in range(5)], gathered)
    join(0, gathered)

    there = has_left.astype(jnp.int32) + has_right.astype(jnp.int32)
    pl.semaphore_wait(barrier, 5 + 4 * there)
    send(0)

    gathered = nothing(3)
    for n, which in enumerate((1, 3, 2)):
        for i in range(cells):
            gathered[n] = lane_pack(lane, gathered[n], coef[which, i], (0, 2, 0)[n] * cells + i)
    wide = [jnp.where(lane % (2 * cells) < cells, g, pltpu.roll(g, cells, 1)) for g in gathered]
    send_c[0] = jnp.where(lane < 2 * cells, wide[0], jnp.where(lane < 4 * cells, wide[1], 0.0))
    send_c[1] = jnp.where(lane < 2 * cells, wide[2], 0.0)
    co_copy().start()
    ct_copy(0).start()
    ct_copy(1).start()
    for way in range(2):
        @pl.when(sides[way][1])
        def _():
            cx_copy(way).start()

    loads[2].wait()
    whole = [(i, CHUNK) for i in range(0, cells, CHUNK)]
    middle = [(i, min(CHUNK, cells - 1 - i)) for i in range(1, cells - 1, CHUNK)]
    ends = [(0, 1), (cells - 1, 1)]

    def first_half(r):
        inner(2 * r)
        known(r)
        receive(r, 0)
        add_x(2 * r)
        outer(2 * r, whole, "plain")
        inner(2 * r + 1)

    def round_(r, carry):
        first_half(r)

        @pl.when(r == 0)
        def _():
            co_copy().wait_recv()
            ct_copy(0).wait_recv()
            ct_copy(1).wait_recv()
            for way in range(2):
                @pl.when(sides[1 - way][1])
                def _():
                    cx_copy(way).wait_recv()

        complete(r)
        receive(r, 1)
        add_x(2 * r + 1)
        gathered = outer(2 * r + 1, middle, "round", nothing(3))
        complete_ends(r)
        gathered = outer(2 * r + 1, ends, "round", gathered)
        join(2 * r + 2, gathered)
        send(r + 1)

        @pl.when(r == 0)
        def _():
            loads[3].wait()

            def weigh(i, carry):
                length = width[i].astype(jnp.float32)
                inverse = 1.0 / (length * length)
                for shift in range(1, SEP + 1):
                    weights[shift - 1, i] = jnp.exp(-(shift * shift) * inverse)
                return carry

            lax.fori_loop(0, cells, weigh, 0)

        return carry

    lax.fori_loop(0, ROUNDS - 1, round_, 0)
    last = ROUNDS - 1
    first_half(last)
    complete(last)
    receive(last, 1)
    add_x(2 * last + 1)
    outer(2 * last + 1, middle, "none")
    for way in range(2):
        @pl.when(sides[way][1])
        def _():
            p_copy(way, 0).start()

    complete_ends(last)
    outer(2 * last + 1, ends, "none")
    for way in range(2):
        @pl.when(sides[way][1])
        def _():
            p_copy(way, 1).start()
            p_copy(way, 2).start()

    stores = [pltpu.make_async_copy(state.at[0, n // 2, n % 2], green[n], store_sem.at[n]) for n in range(10)]
    for store in stores:
        store.start()
    def drain(r, carry):
        for s in (2 * r, 2 * r + 1):
            o_copy(s).wait_send()
            for way in range(2):
                @pl.when(sides[way][1])
                def _():
                    x_copy(s, way).wait_send()

        for way in range(2):
            t_copy(r, 0, way).wait_send()
            t_copy(r, 1, way).wait_send()
            a_copy(r, way).wait_send()

            @pl.when(sides[way][1])
            def _():
                b_copy(r, way).wait_send()
                d_copy(r, way, 0).wait_send()
                d_copy(r, way, 1).wait_send()

        return carry

    lax.fori_loop(0, ROUNDS, drain, 0)
    co_copy().wait_send()
    for way in range(2):
        ct_copy(way).wait_send()

        @pl.when(sides[way][1])
        def _():
            cx_copy(way).wait_send()

    for store in stores:
        store.wait()

    loads[4].wait()
    for way in range(2):
        @pl.when(sides[1 - way][1])
        def _():
            for piece in range(3):
                p_copy(way, piece).wait_recv()

    for i in range(0, cells, CHUNK):
        re, im = (pressure[part, pl.ds(cells + i, CHUNK)] for part in range(2))
        sum_re, sum_im = re, im
        for shift in range(1, SEP + 1):
            w = weights[shift - 1, pl.ds(i, CHUNK)]
            ahead, behind = pl.ds(cells + i + shift, CHUNK), pl.ds(cells + i - shift, CHUNK)
            sum_re = sum_re + w * (pressure[0, ahead] + pressure[0, behind])
            sum_im = sum_im + w * (pressure[1, ahead] + pressure[1, behind])
        result[pl.ds(i, CHUNK)] = amp[pl.ds(i, CHUNK)] * (re * sum_re + im * sum_im)

    last_store = pltpu.make_async_copy(result, intensity, store_sem.at[10])
    last_store.start()

    for way in range(2):
        @pl.when(sides[way][1])
        def _():
            for piece in range(3):
                p_copy(way, piece).wait_send()

    last_store.wait()


def hand_over(*refs):
    fields, (green, intensity, sem) = refs[:11], refs[11:]
    places = [green.at[n // 2, n % 2] for n in range(10)] + [intensity]
    copies = [pltpu.make_async_copy(src, dst, sem.at[n]) for n, (src, dst) in enumerate(zip(fields, places))]
    for copy in copies:
        copy.start()
    for copy in copies:
        copy.wait()


def per_device(n_ax, n_az, adjoint, mean_flow, forcing, tke, half_width, start):
    cells, sector, radial = tke.shape
    block = (cells, sector, radial)
    tile = (sector, radial)
    f32 = jnp.float32
    any_spec = pl.BlockSpec(memory_space=pl.ANY)

    def dma(*shape):
        return pltpu.SemaphoreType.DMA(shape)

    def vmem(*shape):
        return pltpu.VMEM(shape, f32)

    results = pl.pallas_call(
        functools.partial(kernel, n_ax, n_az),
        out_shape=[jax.ShapeDtypeStruct(block, f32)] * 11,
        in_specs=[pl.BlockSpec(memory_space=pltpu.SMEM)] + [any_spec] * 5,
        out_specs=[any_spec] * 11,
        scratch_shapes=[
            vmem(3, 5, 2, *block),
            vmem(5, 2, *block),
            vmem(4, *block),
            vmem(2, *block),
            vmem(*block),
            vmem(*block),
            pltpu.VMEM(block, jnp.int32),
            vmem(SEP, *block),
            vmem(3, *block),
            vmem(*block),
            vmem(5, 2, cells + 2, *tile),
            vmem(SECTIONS, 6, *block),
            vmem(ROUNDS, 4, *block),
            vmem(SECTIONS, 2, 5, 2, *tile),
            vmem(SECTIONS, 2, 5, 2, *tile),
            vmem(SECTIONS, 4, *block),
            vmem(SECTIONS, *tile),
            vmem(SECTIONS, *tile),
            vmem(ROUNDS, 2, 10, *tile),
            vmem(ROUNDS, 2, 10, *tile),
            vmem(ROUNDS, *tile),
            vmem(*tile),
            vmem(ROUNDS, 2, *tile),
            vmem(ROUNDS, 2, *tile),
            vmem(2, 4, *tile),
            vmem(3, *block),
            vmem(2, *tile),
            vmem(2, *tile),
            vmem(2, 3 * cells, *tile),
            dma(5), dma(11),
            dma(SECTIONS, 2), dma(SECTIONS, 2),
            dma(SECTIONS, 2), dma(SECTIONS, 2),
            dma(SECTIONS), dma(SECTIONS),
            dma(2, 3), dma(2, 3),
            dma(ROUNDS, 2, 2), dma(ROUNDS, 2, 2),
            dma(ROUNDS, 2), dma(ROUNDS, 2),
            dma(ROUNDS, 2), dma(ROUNDS, 2),
            dma(2), dma(2),
            dma(2), dma(2),
            dma(1), dma(1),
        ],
        compiler_params=pltpu.CompilerParams(
            collective_id=0, has_side_effects=True, vmem_limit_bytes=54528 * 1024
        ),
    )(start, adjoint, mean_flow, forcing, tke, half_width)
    return pl.pallas_call(
        hand_over,
        out_shape=(
            jax.ShapeDtypeStruct(adjoint.shape, f32),
            jax.ShapeDtypeStruct(tke.shape, f32),
        ),
        in_specs=[any_spec] * 11,
        out_specs=(any_spec, any_spec),
        scratch_shapes=[dma(11)],
        compiler_params=pltpu.CompilerParams(vmem_limit_bytes=2**20),
    )(*results)


def solution(mesh):
    return jax.shard_map(
        functools.partial(per_device, mesh.shape["ax"], mesh.shape["az"]),
        mesh=mesh,
        in_specs=(
            P(None, None, "ax", "az", None),
            P(None, "ax", "az", None),
            P(None, "ax", "az", None),
            P("ax", "az", None),
            P("ax", "az", None),
            P(),
        ),
        out_specs=(P(None, None, "ax", "az", None), P("ax", "az", None)),
        check_vma=False,
    )
```

```python
import functools
import math

import jax
import jax.numpy as jnp
from jax import lax
from jax.experimental import pallas as pl
from jax.experimental.pallas import tpu as pltpu
from jax.sharding import PartitionSpec as P

SEP = 16
SECTIONS = 6
ROUNDS = 3
NAXIAL = 2048
FREQUENCY = 0.7
MESH = pl.DeviceIdType.MESH
CHUNK = 4


def lane_pack(lane, gathered, value, to):
    moved = value if to == 0 else pltpu.roll(value, to, 1)
    return jnp.where(lane == to, moved, gathered)


def kernel(
    n_ax, n_az,
    start, adjoint, mean_flow, forcing, tke, half_width,
    *refs,
):
    green, intensity = refs[:10], refs[10]
    (
        state, partial, coef, force, sigma, amp, width, weights, flow, result,
        flux_x, flux_l, part_l, send_x, recv_x, recv_t, send_o, recv_o,
        send_d, recv_d, recv_a, extra_o, send_p, recv_p, coef_x, coef_t, send_c, coef_o, pressure,
        load_sem, store_sem, x_send, x_recv, t_send, t_recv, o_send, o_recv, p_send, p_recv,
        d_send, d_recv, a_send, a_recv, b_send, b_recv, cx_send, cx_recv, ct_send, ct_recv, co_send, co_recv,
    ) = refs[11:]
    cells, sector, radial = state.shape[3], state.shape[4], state.shape[5]
    ax, az = lax.axis_index("ax"), lax.axis_index("az")
    half_turn = n_az // 2
    left, right = ax - 1, ax + 1
    below, above = lax.rem(az + n_az - 1, n_az), lax.rem(az + 1, n_az)
    opposite = lax.rem(az + half_turn, n_az)
    opposite_below, opposite_above = lax.rem(az + half_turn - 1, n_az), lax.rem(az + half_turn + 1, n_az)
    has_left, has_right = ax > 0, ax < n_ax - 1
    sides = ((right, has_right), (left, has_left))
    turns = ((above, sector - 1, 0), (below, 0, sector - 1))

    loads = [
        pltpu.make_async_copy(src, dst, load_sem.at[n])
        for n, (src, dst) in enumerate(
            [(mean_flow, flow), (adjoint, state.at[0]), (forcing, force), (half_width, width), (tke, amp)]
        )
    ]
    for load in loads:
        load.start()

    barrier = pltpu.get_barrier_semaphore()

    def greet(i, k):
        pl.semaphore_signal(barrier, inc=1, device_id=(i, k), device_id_type=MESH)

    for i, there in sides:
        @pl.when(there)
        def _():
            for k in (opposite, below, above, az):
                greet(i, k)

    for k in (opposite_below, opposite_above, opposite, below, above):
        greet(ax, k)

    step_t = 2 * math.pi / (sector * n_az)
    lane = lax.broadcasted_iota(jnp.int32, (sector, radial), 1)
    row = lax.broadcasted_iota(jnp.int32, (sector, radial), 0)
    radius = lane.astype(jnp.float32) + 0.5
    tau = 0.8 / (2.0 + 1.0 / (radius * step_t))
    turn = 0.5 / (step_t * radius)
    outward = jnp.where(lane == radial - 1, 0.0, 0.5 * (radius + 1.0) / radius)
    inward = jnp.where(lane == 0, 0.0, 0.5 * (radius - 1.0) / radius)
    up = jnp.where(row == sector - 1, 0.0, turn)
    down = jnp.where(row == 0, 0.0, turn)
    is_edge = (row == 0) | (row == sector - 1)
    is_axis = lane == 0
    edge = jnp.where(row == 0, -turn, jnp.where(row == sector - 1, turn, 0.0))
    tau_0 = 0.8 / (2.0 + 1.0 / (0.5 * step_t))
    turn_0 = 0.5 / (step_t * 0.5)
    edge_0 = jnp.where(row == 0, -turn_0, jnp.where(row == sector - 1, turn_0, 0.0))

    first = start[0] + ax * cells
    pos = first + lax.broadcasted_iota(jnp.int32, (cells, sector, radial), 0)
    sigma[...] = 0.5 * (pos.astype(jnp.float32) + 0.5) / NAXIAL

    flux_x[:, :, 0] = jnp.zeros((5, 2, sector, radial), jnp.float32)
    flux_x[:, :, cells + 1] = jnp.zeros((5, 2, sector, radial), jnp.float32)

    @pl.when(jnp.logical_not(has_left))
    def _():
        pressure[:, 0:cells] = jnp.zeros((2, cells, sector, radial), jnp.float32)

    @pl.when(jnp.logical_not(has_right))
    def _():
        pressure[:, 2 * cells : 3 * cells] = jnp.zeros((2, cells, sector, radial), jnp.float32)

    def remote(src, dst, send_sem, recv_sem, i, k):
        return pltpu.make_async_remote_copy(
            src_ref=src, dst_ref=dst, send_sem=send_sem, recv_sem=recv_sem,
            device_id=(i, k), device_id_type=MESH,
        )

    def t_copy(r, later, way):
        who, mine, its = turns[way]
        source = part_l.at[r] if later else flux_l.at[2 * r, pl.ds(0, 4)]
        s = 2 * r + later
        return remote(
            source.at[:, :, mine], recv_t.at[s, :, :, its], t_send.at[s, way], t_recv.at[s, way], ax, who
        )

    def x_copy(s, way):
        return remote(send_x.at[s, way], recv_x.at[s, way], x_send.at[s, way], x_recv.at[s, way], sides[way][0], az)

    def o_copy(s):
        return remote(send_o.at[s], recv_o.at[s], o_send.at[s], o_recv.at[s], ax, opposite)

    def d_copy(r, way, spin):
        who, mine, its = turns[spin]
        return remote(
            send_d.at[r, way, :, mine], recv_d.at[r, way, :, its],
            d_send.at[r, way, spin], d_recv.at[r, way, spin], sides[way][0], who,
        )

    def a_copy(r, spin):
        _, mine, its = turns[spin]
        return remote(
            send_o.at[2 * r, pl.ds(mine, 1)], recv_a.at[r, pl.ds(its, 1)], a_send.at[r, spin], a_recv.at[r, spin],
            ax, (opposite_above, opposite_below)[spin],
        )

    def b_copy(r, way):
        return remote(
            send_p.at[r, way], recv_p.at[r, way], b_send.at[r, way], b_recv.at[r, way], sides[way][0], opposite
        )

    def cx_copy(way):
        return remote(
            coef.at[:, (cells - 1, 0)[way]], coef_x.at[way], cx_send.at[way], cx_recv.at[way], sides[way][0], az
        )

    def ct_copy(way):
        who, mine, its = turns[way]
        return remote(
            coef.at[pl.ds(1, 3), :, mine], coef_t.at[:, :, its], ct_send.at[way], ct_recv.at[way], ax, who
        )

    def co_copy():
        return remote(send_c, coef_o, co_send.at[0], co_recv.at[0], ax, opposite)

    def p_copy(way, piece):
        first, count = ((1, cells - 2), (0, 1), (cells - 1, 1))[piece]
        return remote(
            pressure.at[:, pl.ds(cells + first, count)],
            pressure.at[:, pl.ds((0, 2 * cells)[way] + first, count)],
            p_send.at[way, piece], p_recv.at[way, piece], sides[way][0], az,
        )

    def axial(q, u, rho, stiff, inv):
        a, b, c, d, e = q
        return (u * a, rho * a + stiff * e + u * b, u * c, u * d, b * inv + u * e)

    def fluxes(s, i, q, gathered):
        count = q[0].shape[1]
        at = pl.ds(i, count)
        u, rho, stiff, inv = coef[0, at], coef[1, at], coef[2, at], coef[3, at]
        a, b, c, d, e = q
        shared = rho * a + stiff * e
        turned, spread = d * inv, c * inv
        along = (u * a, shared + u * b, u * c, u * d, b * inv + u * e)
        for n, f in enumerate(along):
            flux_x[n, :, pl.ds(i + 1, count)] = f
        flux_l[s, 0:2, at] = shared
        flux_l[s, 2:4, at] = turned
        flux_l[s, 4:6, at] = spread
        if gathered is None:
            return None
        r = s // 2
        for way, k in ((1, -i), (0, cells - 1 - i)):
            if 0 <= k < count:
                for n, f in enumerate(along):
                    send_x[s, way, n] = f[:, k]
                for n, f in enumerate((along[0], along[3], along[4], shared, turned)):
                    send_d[r, way, 2 * n : 2 * n + 2] = f[:, k]
                packed = jnp.zeros((sector, radial), jnp.float32)
                for n, f in enumerate((shared, spread, along[0], along[2], along[4])):
                    for part in range(2):
                        packed = lane_pack(lane, packed, f[part, k], 2 * n + part)
                send_p[r, way] = packed
        for n, f in enumerate((shared, spread, turned)):
            for part in range(2):
                for k in range(count):
                    gathered[n] = lane_pack(lane, gathered[n], f[part, k], (2 * n + part) * cells + i + k)
        return gathered

    def nothing(count):
        return [jnp.zeros((sector, radial), jnp.float32) for _ in range(count)]

    def known(r):
        s = 2 * r + 1
        gathered = nothing(2)
        for i in range(0, cells, CHUNK):
            at = pl.ds(i, CHUNK)
            rho, stiff, inv = coef[1, at], coef[2, at], coef[3, at]
            shared = rho * partial[0, :, at] + stiff * partial[4, :, at]
            spread = partial[2, :, at] * inv
            part_l[r, 0:2, at] = shared
            part_l[r, 2:4, at] = partial[3, :, at] * inv
            for n, f in enumerate((shared, spread)):
                for part in range(2):
                    for k in range(CHUNK):
                        gathered[n] = lane_pack(lane, gathered[n], f[part, k], (2 * n + part) * cells + i + k)
        send_o[s] = jnp.where(lane < 2 * cells, gathered[0], gathered[1])
        o_copy(s).start()
        t_copy(r, 1, 0).start()
        t_copy(r, 1, 1).start()
        for way, i in ((1, 0), (0, cells - 1)):
            q = [partial[n, :, i] for n in range(5)]
            for n, f in enumerate(axial(q, coef[0, i], coef[1, i], coef[2, i], coef[3, i])):
                send_x[s, way, n] = f
        for way in range(2):
            @pl.when(sides[way][1])
            def _():
                x_copy(s, way).start()

    def send(r):
        for way in range(2):
            @pl.when(sides[way][1])
            def _():
                b_copy(r, way).start()

        a_copy(r, 0).start()
        a_copy(r, 1).start()
        o_copy(2 * r).start()
        for way in range(2):
            @pl.when(sides[way][1])
            def _():
                d_copy(r, way, 0).start()
                d_copy(r, way, 1).start()

        t_copy(r, 0, 0).start()
        t_copy(r, 0, 1).start()
        for way in range(2):
            @pl.when(sides[way][1])
            def _():
                x_copy(2 * r, way).start()

    def weight_of(s):
        third = lax.rem(s, 3)
        return jnp.where(third == 0, 1.0 / 3.0, jnp.where(third == 1, 0.5, 1.0))

    def inner(s):
        source = lax.rem(s, 3)
        scale = weight_of(s) * tau

        half = 0.5 * scale
        turned_by = scale * FREQUENCY

        def radially(f):
            return outward * pltpu.roll(f, radial - 1, 3) - inward * pltpu.roll(f, 1, 3)

        def around(f):
            return up * pltpu.roll(f, sector - 1, 2) - down * pltpu.roll(f, 1, 2)

        for i in range(0, cells, CHUNK):
            at = pl.ds(i, CHUNK)
            fade = scale * sigma[at]
            shared, turned, spread = flux_l[s, 0:2, at], flux_l[s, 2:4, at], flux_l[s, 4:6, at]
            extra = (None, None, radially(shared), around(shared), radially(spread) + around(turned) + force[:, at])
            for n in range(5):
                q = state[source, n, :, at]
                total = state[0, n, :, at] + half * (flux_x[n, :, pl.ds(i + 2, CHUNK)] - flux_x[n, :, at]) - fade * q
                if extra[n] is not None:
                    total = total + scale * extra[n]
                partial[n, 0, at] = total[0] + turned_by * q[1]
                partial[n, 1, at] = total[1] - turned_by * q[0]

    def receive(r, later):
        s = 2 * r + later
        for way in range(2):
            @pl.when(sides[1 - way][1])
            def _():
                x_copy(s, way).wait_recv()

        t_copy(r, later, 0).wait_recv()
        t_copy(r, later, 1).wait_recv()
        o_copy(s).wait_recv()

    def complete(r):
        scale, scale_0 = weight_of(2 * r) * tau, weight_of(2 * r) * tau_0
        half, half_0 = 0.5 * scale, 0.5 * scale_0
        around = scale * edge
        scale_2 = weight_of(2 * r + 1) * tau
        rows = scale_2 * edge
        a_copy(r, 0).wait_recv()
        a_copy(r, 1).wait_recv()
        aside = jnp.where(is_edge, recv_a[r], 0.0)
        axis = -half_0 * aside

        for i in range(0, cells, CHUNK):
            at = pl.ds(i, CHUNK)
            spun = jnp.stack(
                [
                    jnp.stack(
                        [
                            jnp.where(is_axis, pltpu.roll(axis, radial - (2 + part) * cells - i - k, 1), 0.0)
                            for k in range(CHUNK)
                        ]
                    )
                    for part in range(2)
                ]
            )
            more_d = -around * flux_l[2 * r, 0:2, at]
            more_e = spun - around * flux_l[2 * r, 2:4, at]
            partial[3, :, at] = partial[3, :, at] + rows * jnp.where(is_edge, coef_t[1, at] * more_e, 0.0)
            partial[4, :, at] = partial[4, :, at] + rows * jnp.where(is_edge, coef_t[2, at] * more_d, 0.0)

        mine = send_o[2 * r]
        more_c = -half_0 * pltpu.roll(mine, 2 * cells, 1)
        more_e = -half_0 * pltpu.roll(mine, radial - 2 * cells, 1) + scale_0 * edge_0 * pltpu.roll(
            aside, radial - 4 * cells, 1
        )
        extra_o[...] = coef_o[0] * jnp.where(lane < 2 * cells, 0.0, more_c) + coef_o[1] * jnp.where(
            lane < 2 * cells, more_e, 0.0
        )

        for way, i, sign in ((0, 0, 1.0), (1, cells - 1, -1.0)):
            @pl.when(sides[1 - way][1])
            def _():
                d_copy(r, way, 0).wait_recv()
                d_copy(r, way, 1).wait_recv()
                corner = jnp.where(is_edge, recv_d[r, way], 0.0)
                gone = (-sign * half) * corner[0:6]
                more = [(sign * half) * send_x[2 * r, 1 - way, n] for n in range(5)]
                more[3] = more[3] + around * corner[6:8]
                more[4] = more[4] + around * corner[8:10]
                c = coef_x[way]
                along = axial(more, c[0], c[1], c[2], c[3])
                turned = [None, None, None]
                turned += [rows * jnp.where(is_edge, coef_t[0, i] * gone[0:2] + coef_t[1, i] * gone[4:6], 0.0)]
                turned += [rows * jnp.where(is_edge, coef_t[2, i] * gone[2:4], 0.0)]
                for n in range(5):
                    q = partial[n, :, i] - (0.5 * sign * scale_2) * along[n]
                    partial[n, :, i] = q if turned[n] is None else q + turned[n]

    def complete_ends(r):
        half_0 = (0.5 * tau_0) * weight_of(2 * r)
        half = (0.5 * weight_of(2 * r + 1)) * tau
        for way, i, sign in ((0, 0, 1.0), (1, cells - 1, -1.0)):
            @pl.when(sides[1 - way][1])
            def _():
                b_copy(r, way).wait_recv()
                packed = -half_0 * recv_p[r, way]

                def at_axis(n):
                    return jnp.stack(
                        [
                            jnp.where(is_axis, packed if n + part == 0 else pltpu.roll(packed, radial - n - part, 1), 0.0)
                            for part in range(2)
                        ]
                    )

                c, e = (-sign * half) * at_axis(0), (-sign * half) * at_axis(2)
                u, stiff = coef_x[way, 0], coef_x[way, 2]
                partial[1, :, i] = partial[1, :, i] + stiff * e
                partial[2, :, i] = partial[2, :, i] + u * c
                partial[4, :, i] = partial[4, :, i] + u * e

                def spread_out(n, to):
                    low = pltpu.roll(packed, (radial + to + i - n) % radial, 1)
                    high = pltpu.roll(packed, (radial + to + cells + i - n - 1) % radial, 1)
                    return jnp.where(lane == to + i, low, jnp.where(lane == to + cells + i, high, 0.0))

                extra_o[...] = extra_o[...] + sign * (
                    coef_o[0] * (spread_out(4, 0) + spread_out(6, 2 * cells)) + coef_o[1] * spread_out(8, 0)
                )

    def add_x(s):
        half = (0.5 * weight_of(s)) * tau
        for way, i, sign in ((0, 0, -1.0), (1, cells - 1, 1.0)):
            @pl.when(sides[1 - way][1])
            def _():
                partial[:, :, i] = partial[:, :, i] + (sign * half) * recv_x[s, way]

    def outer(s, chunks, then, gathered=None):
        scale = weight_of(s) * tau
        rows = scale * edge
        mirror = recv_o[s] if then == "plain" else recv_o[s] + extra_o[...]
        mirror = (-0.5 * tau_0) * weight_of(s) * mirror
        target = lax.rem(s + 1, 3)
        for i, count in chunks:
            at = pl.ds(i, count)
            q = [partial[n, :, at] for n in range(5)]
            ring = jnp.where(is_edge, recv_t[s, :, at], 0.0) * rows
            spun = [
                jnp.stack(
                    [
                        jnp.stack(
                            [
                                jnp.where(is_axis, pltpu.roll(mirror, (radial - n * cells - i - k) % radial, 1), 0.0)
                                for k in range(count)
                            ]
                        )
                        for n in (c, c + 1)
                    ]
                )
                for c in (0, 2)
            ]
            q[2] = q[2] + spun[0]
            q[3] = q[3] + ring[0:2]
            q[4] = q[4] + ring[2:4] + spun[1]
            for n in range(5):
                state[target, n, :, at] = q[n]
            if then == "none":
                pressure[:, pl.ds(cells + i, count)] = q[4]
            else:
                gathered = fluxes(s + 1, i, q, gathered)
        return gathered

    def join(s, gathered):
        send_o[s] = jnp.where(lane < 2 * cells, gathered[0], jnp.where(lane < 4 * cells, gathered[1], gathered[2]))

    loads[0].wait()
    rho = flow[1]
    coef[0] = flow[0]
    coef[1] = rho
    coef[2] = rho * flow[2]
    coef[3] = 1.0 / rho
    loads[1].wait()
    gathered = nothing(3)
    for i in range(0, cells, CHUNK):
        gathered = fluxes(0, i, [state[0, n, :, pl.ds(i, CHUNK)] for n in range(5)], gathered)
    join(0, gathered)

    there = has_left.astype(jnp.int32) + has_right.astype(jnp.int32)
    pl.semaphore_wait(barrier, 5 + 4 * there)
    send(0)

    gathered = nothing(3)
    for n, which in enumerate((1, 3, 2)):
        for i in range(cells):
            gathered[n] = lane_pack(lane, gathered[n], coef[which, i], (0, 2, 0)[n] * cells + i)
    wide = [jnp.where(lane % (2 * cells) < cells, g, pltpu.roll(g, cells, 1)) for g in gathered]
    send_c[0] = jnp.where(lane < 2 * cells, wide[0], jnp.where(lane < 4 * cells, wide[1], 0.0))
    send_c[1] = jnp.where(lane < 2 * cells, wide[2], 0.0)
    co_copy().start()
    ct_copy(0).start()
    ct_copy(1).start()
    for way in range(2):
        @pl.when(sides[way][1])
        def _():
            cx_copy(way).start()

    loads[2].wait()
    whole = [(i, CHUNK) for i in range(0, cells, CHUNK)]
    middle = [(i, min(CHUNK, cells - 1 - i)) for i in range(1, cells - 1, CHUNK)]
    ends = [(0, 1), (cells - 1, 1)]

    def first_half(r, weighs):
        inner(2 * r)
        known(r)
        if weighs:
            @pl.when(r == 0)
            def _():
                loads[3].wait()

                def weigh(i, carry):
                    length = width[i].astype(jnp.float32)
                    inverse = 1.0 / (length * length)
                    for shift in range(1, SEP + 1):
                        weights[shift - 1, i] = jnp.exp(-(shift * shift) * inverse)
                    return carry

                lax.fori_loop(0, cells, weigh, 0)

        receive(r, 0)
        add_x(2 * r)
        outer(2 * r, whole, "plain")
        inner(2 * r + 1)

    def round_(r, carry):
        first_half(r, True)

        @pl.when(r == 0)
        def _():
            co_copy().wait_recv()
            ct_copy(0).wait_recv()
            ct_copy(1).wait_recv()
            for way in range(2):
                @pl.when(sides[1 - way][1])
                def _():
                    cx_copy(way).wait_recv()

        complete(r)
        receive(r, 1)
        add_x(2 * r + 1)
        gathered = outer(2 * r + 1, middle, "round", nothing(3))
        complete_ends(r)
        gathered = outer(2 * r + 1, ends, "round", gathered)
        join(2 * r + 2, gathered)
        send(r + 1)

        return carry

    lax.fori_loop(0, ROUNDS - 1, round_, 0)
    last = ROUNDS - 1
    first_half(last, False)
    complete(last)
    receive(last, 1)
    add_x(2 * last + 1)
    outer(2 * last + 1, middle, "none")
    for way in range(2):
        @pl.when(sides[way][1])
        def _():
            p_copy(way, 0).start()

    complete_ends(last)
    outer(2 * last + 1, ends, "none")
    for way in range(2):
        @pl.when(sides[way][1])
        def _():
            p_copy(way, 1).start()
            p_copy(way, 2).start()

    stores = [pltpu.make_async_copy(state.at[0, n // 2, n % 2], green[n], store_sem.at[n]) for n in range(10)]
    for store in stores:
        store.start()
    def drain(r, carry):
        for s in (2 * r, 2 * r + 1):
            o_copy(s).wait_send()
            for way in range(2):
                @pl.when(sides[way][1])
                def _():
                    x_copy(s, way).wait_send()

        for way in range(2):
            t_copy(r, 0, way).wait_send()
            t_copy(r, 1, way).wait_send()
            a_copy(r, way).wait_send()

            @pl.when(sides[way][1])
            def _():
                b_copy(r, way).wait_send()
                d_copy(r, way, 0).wait_send()
                d_copy(r, way, 1).wait_send()

        return carry

    lax.fori_loop(0, ROUNDS, drain, 0)
    co_copy().wait_send()
    for way in range(2):
        ct_copy(way).wait_send()

        @pl.when(sides[way][1])
        def _():
            cx_copy(way).wait_send()

    for store in stores:
        store.wait()

    loads[4].wait()
    for way in range(2):
        @pl.when(sides[1 - way][1])
        def _():
            for piece in range(3):
                p_copy(way, piece).wait_recv()

    for i in range(0, cells, CHUNK):
        re, im = (pressure[part, pl.ds(cells + i, CHUNK)] for part in range(2))
        sum_re, sum_im = re, im
        for shift in range(1, SEP + 1):
            w = weights[shift - 1, pl.ds(i, CHUNK)]
            ahead, behind = pl.ds(cells + i + shift, CHUNK), pl.ds(cells + i - shift, CHUNK)
            sum_re = sum_re + w * (pressure[0, ahead] + pressure[0, behind])
            sum_im = sum_im + w * (pressure[1, ahead] + pressure[1, behind])
        result[pl.ds(i, CHUNK)] = amp[pl.ds(i, CHUNK)] * (re * sum_re + im * sum_im)

    last_store = pltpu.make_async_copy(result, intensity, store_sem.at[10])
    last_store.start()

    for way in range(2):
        @pl.when(sides[way][1])
        def _():
            for piece in range(3):
                p_copy(way, piece).wait_send()

    last_store.wait()


def hand_over(*refs):
    fields, (green, intensity, sem) = refs[:11], refs[11:]
    places = [green.at[n // 2, n % 2] for n in range(10)] + [intensity]
    copies = [pltpu.make_async_copy(src, dst, sem.at[n]) for n, (src, dst) in enumerate(zip(fields, places))]
    for copy in copies:
        copy.start()
    for copy in copies:
        copy.wait()


def per_device(n_ax, n_az, adjoint, mean_flow, forcing, tke, half_width, start):
    cells, sector, radial = tke.shape
    block = (cells, sector, radial)
    tile = (sector, radial)
    f32 = jnp.float32
    any_spec = pl.BlockSpec(memory_space=pl.ANY)

    def dma(*shape):
        return pltpu.SemaphoreType.DMA(shape)

    def vmem(*shape):
        return pltpu.VMEM(shape, f32)

    results = pl.pallas_call(
        functools.partial(kernel, n_ax, n_az),
        out_shape=[jax.ShapeDtypeStruct(block, f32)] * 11,
        in_specs=[pl.BlockSpec(memory_space=pltpu.SMEM)] + [any_spec] * 5,
        out_specs=[any_spec] * 11,
        scratch_shapes=[
            vmem(3, 5, 2, *block),
            vmem(5, 2, *block),
            vmem(4, *block),
            vmem(2, *block),
            vmem(*block),
            vmem(*block),
            pltpu.VMEM(block, jnp.int32),
            vmem(SEP, *block),
            vmem(3, *block),
            vmem(*block),
            vmem(5, 2, cells + 2, *tile),
            vmem(SECTIONS, 6, *block),
            vmem(ROUNDS, 4, *block),
            vmem(SECTIONS, 2, 5, 2, *tile),
            vmem(SECTIONS, 2, 5, 2, *tile),
            vmem(SECTIONS, 4, *block),
            vmem(SECTIONS, *tile),
            vmem(SECTIONS, *tile),
            vmem(ROUNDS, 2, 10, *tile),
            vmem(ROUNDS, 2, 10, *tile),
            vmem(ROUNDS, *tile),
            vmem(*tile),
            vmem(ROUNDS, 2, *tile),
            vmem(ROUNDS, 2, *tile),
            vmem(2, 4, *tile),
            vmem(3, *block),
            vmem(2, *tile),
            vmem(2, *tile),
            vmem(2, 3 * cells, *tile),
            dma(5), dma(11),
            dma(SECTIONS, 2), dma(SECTIONS, 2),
            dma(SECTIONS, 2), dma(SECTIONS, 2),
            dma(SECTIONS), dma(SECTIONS),
            dma(2, 3), dma(2, 3),
            dma(ROUNDS, 2, 2), dma(ROUNDS, 2, 2),
            dma(ROUNDS, 2), dma(ROUNDS, 2),
            dma(ROUNDS, 2), dma(ROUNDS, 2),
            dma(2), dma(2),
            dma(2), dma(2),
            dma(1), dma(1),
        ],
        compiler_params=pltpu.CompilerParams(
            collective_id=0, has_side_effects=True, vmem_limit_bytes=54528 * 1024
        ),
    )(start, adjoint, mean_flow, forcing, tke, half_width)
    return pl.pallas_call(
        hand_over,
        out_shape=(
            jax.ShapeDtypeStruct(adjoint.shape, f32),
            jax.ShapeDtypeStruct(tke.shape, f32),
        ),
        in_specs=[any_spec] * 11,
        out_specs=(any_spec, any_spec),
        scratch_shapes=[dma(11)],
        compiler_params=pltpu.CompilerParams(vmem_limit_bytes=2**20),
    )(*results)


def solution(mesh):
    return jax.shard_map(
        functools.partial(per_device, mesh.shape["ax"], mesh.shape["az"]),
        mesh=mesh,
        in_specs=(
            P(None, None, "ax", "az", None),
            P(None, "ax", "az", None),
            P(None, "ax", "az", None),
            P("ax", "az", None),
            P("ax", "az", None),
            P(),
        ),
        out_specs=(P(None, None, "ax", "az", None), P("ax", "az", None)),
        check_vma=False,
    )
```
